32 devices in a mesh: groups: 2 (over x), seq: 16 (over z, y, core).
Axes of the slice: x: 2, y: 2, z: 4, core: 2. Of those that a mesh axis runs over, the one named last changes fastest.
Arguments:
- features: bfloat16 [4096, 2048], P(('groups', 'seq')), parts along dimension 0, may hold values from -40 to 40
- state_write: bfloat16 [4096, 64], P(('groups', 'seq')), parts along dimension 0, may hold values from -0.75 to 0.75
- state_read: bfloat16 [4096, 64], P(('groups', 'seq')), parts along dimension 0, may hold values from -0.75 to 0.75
- log_decay: float32 [4096, 32], P(('groups', 'seq')), parts along dimension 0, may hold values from -2 to 0
- skip_gain: float32 [32], replicated, may hold values from 1 to 4
- post_gain: float32 [2048], replicated, may hold values from 0.5 to 2
- start_index: int32 [4096], P(('groups', 'seq')), parts along dimension 0, may hold values from 0 to 2047, as said below
- step_noise: bfloat16 [3, 4096, 1024], P(None, ('groups', 'seq')), parts along dimension 1, may hold values from -4 to 4
- act_weight: bfloat16 [2048, 128], replicated, may hold values from -0.125 to 0.125
- dyn_weight: bfloat16 [2048, 1024], replicated, may hold values from -0.125 to 0.125
- act_in_weight: bfloat16 [128, 1024], replicated, may hold values from -0.5 to 0.5
- out_weight: bfloat16 [1024, 2048], replicated, may hold values from -0.1875 to 0.1875
- value_weight: bfloat16 [1024], replicated, may hold values from -0.1875 to 0.1875
Outputs:
- posterior: bfloat16 [4096, 2048], P(('groups', 'seq')), parts along dimension 0
- values: float32 [3, 4096], P(None, ('groups', 'seq')), parts along dimension 1
- final_latent: bfloat16 [4096, 2048], P(('groups', 'seq')), parts along dimension 0
The draws below stay inside these ranges and needn't reach their ends.
There are 2 independent parts, one for each index of `groups`. The reference program is written for one: setup_inputs(seed, part) draws one part's arguments, and reference() takes and returns one part's arrays. A program takes and returns all parts, laid end to end along the dimension named above; an argument that names none is the same for every part. Nothing has to cross between parts.
Inputs may be any that keep to these rules, and one draw needn't show every extreme that they name: `start_index`: each aligned block of 128 starts (the starts of one device) names exactly 8 time steps in every aligned range of 128 time steps.
All inputs are finite; a program needn't handle non-finite values.
Results may differ from the reference program's by a relative error of at most 0.01.
Values may be sent and summed in bfloat16 or wider, within the bound.
A program may use at most 192 MiB of HBM per device.

```python
import math
import jax
import jax.numpy as jnp
from jax import lax

D = 2048
HEAD_DIM = 64
STATE = 64
HID = 1024
ACT = 128
HORIZON = 3
TOK_DEV = 128
STARTS_DEV = 128
HEAD_TOTAL = 32
TOKEN_STEPS = 2048
STARTS = 2048
CAP = 8


def draw_features(key, part):
    random_keys = jax.random.split(key, 3)
    row_scale = jnp.exp(jax.random.uniform(random_keys[0], (TOKEN_STEPS, 1), minval=0.0, maxval=jnp.log(10.0)))
    col_scale = jnp.exp(jax.random.uniform(random_keys[1], (1, D), minval=0.0, maxval=jnp.log(10.0)))
    base = jnp.clip(jax.random.normal(random_keys[2], (TOKEN_STEPS, D)), -4.0, 4.0)
    return (base * row_scale * col_scale / 10.0).astype(jnp.bfloat16)


def draw_log_decay(key, part):
    random_keys = jax.random.split(key, 5)
    fast = jax.random.uniform(random_keys[0], (HEAD_TOTAL,)) < 0.5
    fast_rate = jnp.exp(jax.random.uniform(random_keys[1], (HEAD_TOTAL,), minval=jnp.log(1.0 / 50.0), maxval=jnp.log(1.0 / 30.0)))
    slow_rate = 0.3 / TOKEN_STEPS
    baseline_rate = jnp.where(fast, fast_rate, slow_rate)
    coarse_value = jnp.exp(jax.random.uniform(random_keys[2], (TOKEN_STEPS, HEAD_TOTAL), minval=-0.7, maxval=0.7))
    spike_rows = jax.random.randint(random_keys[3], (3,), 0, TOKEN_STEPS)
    spike_loss = jax.random.uniform(random_keys[4], (3, HEAD_TOTAL), minval=0.2, maxval=0.5)
    token_positions = jnp.arange(TOKEN_STEPS, dtype=jnp.int32)
    matched_rows = (token_positions[:, None] == spike_rows[None, :]).astype(jnp.float32)
    spike_events = jnp.sum(matched_rows[:, :, None] * jnp.log1p(-spike_loss)[None, :, :], axis=1)
    return (-baseline_rate[None, :] * coarse_value + spike_events).astype(jnp.float32)


def draw_start_index(key, part):
    block_count = STARTS // STARTS_DEV
    random_keys = jax.random.split(key, 2)
    slot_ids = jnp.arange(STARTS_DEV, dtype=jnp.int32)
    owners = jnp.broadcast_to((slot_ids // CAP)[None, :], (block_count, STARTS_DEV))
    perm_keys = jax.random.split(random_keys[0], block_count)
    shuffles = jax.vmap(lambda one_key: jax.random.permutation(one_key, STARTS_DEV))(perm_keys)
    owners = jnp.take_along_axis(owners, shuffles.astype(jnp.int32), axis=1)
    offsets = jax.random.randint(random_keys[1], (block_count, STARTS_DEV), 0, TOK_DEV)
    return (owners * TOK_DEV + offsets).reshape(STARTS).astype(jnp.int32)


def steps_of(own_key, shape, shards, smallest, top_value):
    level, own = 1.0, jax.random.fold_in(own_key, 6)
    for axis_at, shards_of in shards:
        heights = jnp.exp(jax.random.uniform(jax.random.fold_in(own, axis_at), (shards_of,), jnp.float32, smallest / len(shards), top_value / len(shards)))
        level = level * jnp.repeat(heights, shape[axis_at] // shards_of).reshape([-1 if axis == axis_at else 1 for axis in range(len(shape))])
    return level


def noise(key, extent, deviation, limit, cuts=(), held_as=jnp.bfloat16):
    gain = steps_of(key, extent, cuts, -0.22, 0.18) if cuts else 1.0
    entries = jax.random.normal(key, extent, jnp.float32) * deviation * gain
    return jnp.minimum(jnp.maximum(entries, -limit), limit).astype(held_as)


def setup_inputs(seed: int = 0, part: int = 0) -> dict:
    splits = jax.random.split(jax.random.key(seed), 14)
    part_keys = jax.random.split(jax.random.fold_in(splits[13], part), 14)
    features = draw_features(jax.random.fold_in(jax.random.fold_in(splits[13], part), 71), part)
    state_write = noise(part_keys[1], (TOKEN_STEPS, STATE), STATE ** -0.5, 0.75, ((0, 16),))
    state_read = noise(part_keys[2], (TOKEN_STEPS, STATE), STATE ** -0.5, 0.75, ((0, 16),))
    log_decay = draw_log_decay(jax.random.fold_in(jax.random.fold_in(splits[13], part), 71), part)
    skip_gain = jnp.clip(jnp.exp(jax.random.uniform(splits[4], (HEAD_TOTAL,), jnp.float32, math.log(1.0), math.log(4.0))), 1.0, 4.0)
    post_gain = jnp.clip(jnp.exp(jax.random.uniform(splits[5], (D,), jnp.float32, math.log(0.5), math.log(2.0))), 0.5, 2.0)
    start_index = draw_start_index(jax.random.fold_in(jax.random.fold_in(splits[13], part), 71), part)
    step_noise = noise(part_keys[7], (HORIZON, STARTS, HID), 1.0, 4.0, ((1, 16),))
    act_weight = noise(splits[8], (D, ACT), D ** -0.5, 0.125)
    dyn_weight = noise(splits[9], (D, HID), D ** -0.5, 0.125)
    act_in_weight = noise(splits[10], (ACT, HID), ACT ** -0.5, 0.5)
    out_weight = noise(splits[11], (HID, D), HID ** -0.5, 0.1875)
    value_weight = noise(splits[12], (HID,), HID ** -0.5, 0.1875)
    return dict(features=features, state_write=state_write, state_read=state_read, log_decay=log_decay, skip_gain=skip_gain, post_gain=post_gain, start_index=start_index, step_noise=step_noise, act_weight=act_weight, dyn_weight=dyn_weight, act_in_weight=act_in_weight, out_weight=out_weight, value_weight=value_weight)


def reference(features, state_write, state_read, log_decay, skip_gain, post_gain, start_index, step_noise, act_weight, dyn_weight, act_in_weight, out_weight, value_weight):
    heads_in = features.astype(jnp.float32).reshape(TOKEN_STEPS, HEAD_TOTAL, HEAD_DIM)
    write_in = state_write.astype(jnp.float32)
    read_in = state_read.astype(jnp.float32)

    def advance(state_now, inputs):
        x_row, write_row, read_row, decay_row = inputs
        state_next = jnp.exp(decay_row)[:, None, None] * state_now + x_row[:, :, None] * write_row[None, None, :]
        read_out = jnp.einsum('hpn,n->hp', state_next, read_row, precision=lax.Precision.HIGHEST)
        return (state_next, read_out)
    start_state = jnp.zeros((HEAD_TOTAL, HEAD_DIM, STATE), jnp.float32)
    _, read_all = lax.scan(advance, start_state, (heads_in, write_in, read_in, log_decay))
    mixed = read_all + skip_gain[None, :, None] * heads_in
    square_mean = lax.optimization_barrier(jnp.mean(mixed * mixed, axis=-1, keepdims=True))
    normed_heads = mixed * lax.rsqrt(square_mean + 1e-05) * post_gain.reshape(HEAD_TOTAL, HEAD_DIM)[None]
    posterior = normed_heads.reshape(TOKEN_STEPS, D).astype(jnp.bfloat16)
    latent = jnp.take(posterior, start_index, axis=0)
    value_list = []
    for step_idx in range(HORIZON):
        wide = latent.astype(jnp.float32)
        normed = (wide * lax.rsqrt(lax.optimization_barrier(jnp.mean(wide * wide, axis=-1, keepdims=True)) + 1e-06)).astype(jnp.bfloat16)
        action = jnp.tanh(jnp.dot(normed, act_weight, preferred_element_type=jnp.float32)).astype(jnp.bfloat16)
        inner = jnp.dot(normed, dyn_weight, preferred_element_type=jnp.float32) + jnp.dot(action, act_in_weight, preferred_element_type=jnp.float32)
        hidden = (jax.nn.silu(inner) + step_noise[step_idx].astype(jnp.float32)).astype(jnp.bfloat16)
        value_list.append(jnp.dot(hidden, value_weight, preferred_element_type=jnp.float32))
        latent = (wide + jnp.dot(hidden, out_weight, preferred_element_type=jnp.float32)).astype(jnp.bfloat16)
    return (posterior, jnp.stack(value_list), latent)
```

```python
import functools
import jax
import jax.numpy as jnp
from jax import lax
from jax.experimental import pallas as pl
from jax.experimental.pallas import tpu as pltpu
from jax.sharding import PartitionSpec as P

F32 = jnp.float32
BF16 = jnp.bfloat16


def dot(a, b):
    return jnp.dot(a, b, preferred_element_type=F32)


def dot_nt(a, b):
    return lax.dot_general(a, b, (((1,), (1,)), ((), ())), preferred_element_type=F32)


def iota(shape, dim):
    return lax.broadcasted_iota(jnp.int32, shape, dim)


def plan(n, rows, width, state, starts):
    lanes = max(128, width // n)
    lane_blocks = width // lanes
    cuts = min(state // 16, n // lane_blocks)
    cap = starts // n
    pieces = max(1, 16 // cap)
    return lanes, lane_blocks, cuts, cap, pieces


def kernel(
    n,
    x_ref,
    write_ref,
    read_ref,
    decay_ref,
    skip_ref,
    gain_ref,
    start_ref,
    value_w_ref,
    noise_hbm,
    act_hbm,
    dyn_hbm,
    act_in_hbm,
    out_hbm,
    post_hbm,
    values_ref,
    final_hbm,
    noise,
    act_w,
    dyn_w,
    act_in_w,
    out_w,
    meta_out,
    meta_in,
    end_out,
    end_in,
    carry_out,
    carry_in,
    local,
    entered,
    post,
    pick_out,
    pick_in,
    latent,
    load_sem,
    post_sem,
    meta_s,
    meta_r,
    end_s,
    end_r,
    carry_s,
    carry_r,
    pick_s,
    pick_r,
):
    rows, width = x_ref.shape
    heads = decay_ref.shape[1]
    head_width = width // heads
    state = write_ref.shape[1]
    starts = start_ref.shape[1]
    lanes, lane_blocks, cuts, cap, pieces = plan(n, rows, width, state, starts)
    owners = lane_blocks * cuts
    depth = state // cuts
    slot_rows = pieces * cap
    piece_width = width // pieces
    me = lax.axis_index("seq")

    loads = [
        pltpu.make_async_copy(src, dst, load_sem.at[i])
        for i, (src, dst) in enumerate(
            (
                (act_hbm, act_w),
                (dyn_hbm, dyn_w),
                (act_in_hbm, act_in_w),
                (out_hbm, out_w),
                (noise_hbm, noise),
            )
        )
    ]
    for load in loads:
        load.start()

    barrier = pltpu.get_barrier_semaphore()

    def greet(j, _):
        pl.semaphore_signal(
            barrier,
            inc=1,
            device_id={"seq": lax.rem(me + j, n)},
            device_id_type=pl.DeviceIdType.MESH,
        )
        return 0

    lax.fori_loop(1, n, greet, 0)

    def remote(src, dst, send, recv, peer, slot):
        return pltpu.make_async_remote_copy(
            src_ref=src,
            dst_ref=dst,
            send_sem=send.at[peer],
            recv_sem=recv.at[slot],
            device_id={"seq": peer},
            device_id_type=pl.DeviceIdType.MESH,
        )

    lower = iota((rows, rows), 0) >= iota((rows, rows), 1)
    running = jnp.dot(
        lower.astype(F32),
        decay_ref[...],
        precision=lax.Precision.HIGHEST,
        preferred_element_type=F32,
    )
    spread = (iota((heads, width), 1) // head_width == iota((heads, width), 0)).astype(BF16)

    def widen(v):
        high = v.astype(BF16)
        low = (v - high.astype(F32)).astype(BF16)
        return dot(high, spread) + dot(low, spread)

    x_all = x_ref[...].astype(F32)
    tail = widen(jnp.exp(running[rows - 1 : rows] - running))
    eye_state = (iota((state, state), 0) == iota((state, state), 1)).astype(BF16)
    write_t = dot_nt(eye_state, write_ref[...]).astype(BF16)
    end_state = dot(write_t, (x_all * tail).astype(BF16))
    whole_decay = widen(jnp.exp(running[rows - 8 : rows]))[7:8]
    start_row = start_ref[...].astype(F32)
    for k in range(owners):
        at = slice((k // cuts) * lanes, (k // cuts + 1) * lanes)
        end_out[k] = end_state[(k % cuts) * depth : (k % cuts + 1) * depth, at].astype(BF16)
    meta_width = meta_out.shape[2]

    def padded(row):
        if row.shape[1] == meta_width:
            return row
        return jnp.concatenate([row, jnp.zeros((1, meta_width - row.shape[1]), F32)], axis=1)

    for k in range(n):
        block = min(k // cuts, lane_blocks - 1)
        meta_out[k, 0:1, :] = padded(start_row)
        meta_out[k, 1:2, :] = padded(whole_decay[:, block * lanes : (block + 1) * lanes])

    pl.semaphore_wait(barrier, n - 1)

    def send_first(j, _):
        peer = lax.rem(me + j, n)

        def send_end():
            remote(end_out.at[peer], end_in.at[me], end_s, end_r, peer, me).start()

        remote(meta_out.at[peer], meta_in.at[me], meta_s, meta_r, peer, me).start()
        if owners == n:
            send_end()
        else:
            pl.when(peer < owners)(send_end)
        return 0

    lax.fori_loop(1, n, send_first, 0)
    meta_in[pl.ds(me, 1)] = meta_out[pl.ds(me, 1)]

    def keep_own():
        end_in[pl.ds(me, 1)] = end_out[pl.ds(me, 1)]

    if owners == n:
        keep_own()
    else:
        pl.when(me < owners)(keep_own)

    running_t = running.T
    gram = dot_nt(read_ref[...], write_ref[...])
    skip = widen(jnp.broadcast_to(skip_ref[...], (8, heads)))[0:1]
    per_tile = 128 // head_width
    head_of = iota((rows, 128), 1) // head_width
    for tile in range(width // 128):
        at = slice(tile * 128, (tile + 1) * 128)
        x_tile = x_ref[:, at]
        total = x_tile.astype(F32) * skip[:, at]
        for inner in range(per_tile):
            h = tile * per_tile + inner
            gap = running[:, h : h + 1] - running_t[h : h + 1, :]
            weight = (jnp.exp(jnp.where(lower, gap, -jnp.inf)) * gram).astype(BF16)
            one_head = jnp.where(head_of == inner, x_tile.astype(F32), 0.0).astype(BF16)
            total = total + dot(weight, one_head)
        local[:, at] = total
    entered[...] = widen(jnp.exp(running))

    def fold():
        def lap(d, carry):
            carry_out[d] = carry.astype(BF16)

            @pl.when(d != me)
            def _():
                remote(carry_out.at[d], carry_in.at[me], carry_s, carry_r, d, me).start()
                remote(end_out.at[0], end_in.at[d], end_s, end_r, d, d).wait_recv()
                remote(meta_out.at[0], meta_in.at[d], meta_s, meta_r, d, d).wait_recv()

            return carry * meta_in[d, 1:2, :lanes] + end_in[d].astype(F32)

        lax.fori_loop(0, n, lap, jnp.zeros((depth, lanes), F32))
        carry_in[pl.ds(me, 1)] = carry_out[pl.ds(me, 1)]

    def only_meta():
        def lap(d, _):
            @pl.when(d != me)
            def _():
                remote(meta_out.at[0], meta_in.at[d], meta_s, meta_r, d, d).wait_recv()

            return 0

        lax.fori_loop(0, n, lap, 0)

    if owners == n:
        fold()
    else:
        pl.when(me < owners)(fold)
        pl.when(me >= owners)(only_meta)

    asked = meta_in[:, 0, :starts]
    base = (me * rows).astype(F32)
    hit = jnp.logical_and(asked >= base, asked < base + rows)
    up_to = (iota((starts, starts), 0) <= iota((starts, starts), 1)).astype(BF16)
    rank = dot(hit.astype(F32).astype(BF16), up_to)
    rank = jnp.where(hit, rank, 0.0).astype(BF16)
    offset = jnp.where(hit, asked - base, 0.0).astype(BF16)
    slots = n * slot_rows
    repeat = (iota((slots, n), 0) // slot_rows == iota((slots, n), 1)).astype(BF16)
    slot_at = iota((slots, starts), 0)
    chosen = dot(repeat, rank) == (slot_at % cap + 1).astype(F32)
    wanted = jnp.sum(jnp.where(chosen, dot(repeat, offset), 0.0), axis=1, keepdims=True)
    row_at = iota((slots, rows), 0)
    picks_row = wanted == iota((slots, rows), 1).astype(F32)
    picks = [
        jnp.where(jnp.logical_and(picks_row, (row_at // cap) % pieces == p), 1.0, 0.0).astype(BF16)
        for p in range(pieces)
    ]

    start_col = jnp.sum(
        jnp.where(iota((starts, starts), 0) == iota((starts, starts), 1), start_row, 0.0),
        axis=1,
        keepdims=True,
    )
    first = (iota((starts, n), 1) * rows).astype(F32)
    from_owner = jnp.logical_and(start_col >= first, start_col < first + rows)
    before = (iota((starts, starts), 0) >= iota((starts, starts), 1)).astype(BF16)
    count = dot(before, from_owner.astype(F32).astype(BF16))
    lands = jnp.sum(
        jnp.where(from_owner, count - 1.0 + (iota((starts, n), 1) * slot_rows).astype(F32), 0.0),
        axis=1,
        keepdims=True,
    )

    def carry_lap(k, _):
        @pl.when(k != me)
        def _():
            remote(carry_out.at[0], carry_in.at[k], carry_s, carry_r, k, k).wait_recv()

        return 0

    lax.fori_loop(0, owners, carry_lap, 0)
    same_head = jnp.where(
        iota((lanes, lanes), 0) // head_width == iota((lanes, lanes), 1) // head_width,
        1.0 / head_width,
        0.0,
    ).astype(BF16)
    read = read_ref[...]
    for block in range(lane_blocks):
        at = slice(block * lanes, (block + 1) * lanes)
        carry = carry_in[block * cuts : (block + 1) * cuts].reshape(state, lanes)
        mixed = local[:, at] + dot(read, carry) * entered[:, at]
        square_mean = dot((mixed * mixed).astype(BF16), same_head)
        post[:, at] = (mixed * lax.rsqrt(square_mean + 1e-05) * gain_ref[:, at]).astype(BF16)
    picked = dot(picks[0], post[:, :piece_width])
    for p in range(1, pieces):
        picked = picked + dot(picks[p], post[:, p * piece_width : (p + 1) * piece_width])
    pick_out[...] = picked.astype(BF16).reshape(n, slot_rows, piece_width)

    def send_rows(j, _):
        peer = lax.rem(me + j, n)
        remote(pick_out.at[peer], pick_in.at[me], pick_s, pick_r, peer, me).start()
        return 0

    lax.fori_loop(1, n, send_rows, 0)
    pick_in[pl.ds(me, 1)] = pick_out[pl.ds(me, 1)]
    post_copy = pltpu.make_async_copy(post, post_hbm, post_sem.at[0])
    post_copy.start()
    for load in loads:
        load.wait()

    def row_lap(j, _):
        peer = lax.rem(me + j, n)
        remote(pick_out.at[0], pick_in.at[peer], pick_s, pick_r, peer, peer).wait_recv()
        return 0

    lax.fori_loop(1, n, row_lap, 0)

    landed = pick_in[...].reshape(slots, piece_width)
    slot_of = iota((starts, slots), 1).astype(F32)
    for p in range(pieces):
        place = jnp.where(slot_of == lands + float(p * cap), 1.0, 0.0).astype(BF16)
        latent[:, p * piece_width : (p + 1) * piece_width] = dot(place, landed).astype(BF16)

    diagonal = iota((starts, starts), 0) == iota((starts, starts), 1)
    value_w = value_w_ref[...].astype(F32)
    for step in range(noise.shape[0]):
        wide = latent[...].astype(F32)
        normed = (
            wide * lax.rsqrt(jnp.mean(wide * wide, axis=-1, keepdims=True) + 1e-06)
        ).astype(BF16)
        action = jnp.tanh(dot(normed, act_w[...])).astype(BF16)
        inner = dot(normed, dyn_w[...]) + dot(action, act_in_w[...])
        hidden = (inner / (1.0 + jnp.exp(-inner)) + noise[step].astype(F32)).astype(BF16)
        value = jnp.sum(hidden.astype(F32) * value_w, axis=1, keepdims=True)
        values_ref[step : step + 1, :] = jnp.sum(
            jnp.where(diagonal, value, 0.0), axis=0, keepdims=True
        )
        latent[...] = (wide + dot(hidden, out_w[...])).astype(BF16)

    final_copy = pltpu.make_async_copy(latent, final_hbm, post_sem.at[1])
    final_copy.start()

    def sent(j, _):
        peer = lax.rem(me + j, n)
        remote(meta_out.at[0], meta_in.at[me], meta_s, meta_r, peer, me).wait_send()
        remote(pick_out.at[0], pick_in.at[me], pick_s, pick_r, peer, me).wait_send()

        def end_sent():
            remote(end_out.at[0], end_in.at[me], end_s, end_r, peer, me).wait_send()

        def carry_sent():
            remote(carry_out.at[0], carry_in.at[me], carry_s, carry_r, peer, me).wait_send()

        if owners == n:
            end_sent()
            carry_sent()
        else:
            pl.when(peer < owners)(end_sent)
            pl.when(me < owners)(carry_sent)
        return 0

    lax.fori_loop(1, n, sent, 0)
    post_copy.wait()
    final_copy.wait()


def per_device(
    features,
    state_write,
    state_read,
    log_decay,
    skip_gain,
    post_gain,
    start_index,
    step_noise,
    act_weight,
    dyn_weight,
    act_in_weight,
    out_weight,
    value_weight,
):
    n = lax.axis_size("seq")
    rows, width = features.shape
    state = state_write.shape[1]
    starts = start_index.shape[0]
    lanes, lane_blocks, cuts, cap, pieces = plan(n, rows, width, state, starts)
    owners, depth, slot_rows = lane_blocks * cuts, state // cuts, pieces * cap
    vmem = pl.BlockSpec(memory_space=pltpu.VMEM)
    hbm = pl.BlockSpec(memory_space=pl.ANY)
    sems = pltpu.SemaphoreType.DMA((n,))
    flops = 2 * step_noise.shape[0] * starts * (dyn_weight.size + out_weight.size)
    return pl.pallas_call(
        functools.partial(kernel, n),
        out_shape=(
            jax.ShapeDtypeStruct((rows, width), BF16),
            jax.ShapeDtypeStruct((step_noise.shape[0], starts), F32),
            jax.ShapeDtypeStruct((starts, width), BF16),
        ),
        in_specs=[vmem] * 8 + [hbm] * 5,
        out_specs=(hbm, vmem, hbm),
        scratch_shapes=[
            pltpu.VMEM(step_noise.shape, BF16),
            pltpu.VMEM(act_weight.shape, BF16),
            pltpu.VMEM(dyn_weight.shape, BF16),
            pltpu.VMEM(act_in_weight.shape, BF16),
            pltpu.VMEM(out_weight.shape, BF16),
            pltpu.VMEM((n, 8, max(lanes, starts)), F32),
            pltpu.VMEM((n, 8, max(lanes, starts)), F32),
            pltpu.VMEM((owners, depth, lanes), BF16),
            pltpu.VMEM((n, depth, lanes), BF16),
            pltpu.VMEM((n, depth, lanes), BF16),
            pltpu.VMEM((owners, depth, lanes), BF16),
            pltpu.VMEM((rows, width), F32),
            pltpu.VMEM((rows, width), F32),
            pltpu.VMEM((rows, width), BF16),
            pltpu.VMEM((n, slot_rows, width // pieces), BF16),
            pltpu.VMEM((n, slot_rows, width // pieces), BF16),
            pltpu.VMEM((starts, width), BF16),
            pltpu.SemaphoreType.DMA((5,)),
            pltpu.SemaphoreType.DMA((2,)),
            sems,
            sems,
            sems,
            sems,
            sems,
            sems,
            sems,
            sems,
        ],
        compiler_params=pltpu.CompilerParams(
            collective_id=0, has_side_effects=True, vmem_limit_bytes=56 * 1024 * 1024
        ),
        cost_estimate=pl.CostEstimate(
            flops=flops, bytes_accessed=12 * 1024 * 1024, transcendentals=1024 * 1024
        ),
    )(
        features,
        state_write,
        state_read,
        log_decay,
        skip_gain[None, :],
        post_gain[None, :],
        start_index[None, :],
        value_weight[None, :],
        step_noise,
        act_weight,
        dyn_weight,
        act_in_weight,
        out_weight,
    )


def solution(mesh):
    split = P(("groups", "seq"), None)
    placed = (
        split,
        split,
        split,
        split,
        P(),
        P(),
        P(("groups", "seq")),
        P(None, ("groups", "seq"), None),
        P(),
        P(),
        P(),
        P(),
        P(),
    )
    return jax.shard_map(
        per_device,
        mesh=mesh,
        in_specs=placed,
        out_specs=(split, P(None, ("groups", "seq")), split),
        check_vma=False,
    )
```

```python
import functools
import jax
import jax.numpy as jnp
from jax import lax
from jax.experimental import pallas as pl
from jax.experimental.pallas import tpu as pltpu
from jax.sharding import PartitionSpec as P

F32 = jnp.float32
BF16 = jnp.bfloat16
VMEM_LIMIT = 56 * 1024 * 1024


def dot(a, b):
    return jnp.dot(a, b, preferred_element_type=F32)


def dot_nt(a, b):
    return lax.dot_general(a, b, (((1,), (1,)), ((), ())), preferred_element_type=F32)


def iota(shape, dim):
    return lax.broadcasted_iota(jnp.int32, shape, dim)


def plan(n, rows, width, state, starts):
    half = n // 2
    lanes = max(128, width // half)
    lane_blocks = width // lanes
    cuts = min(state // 16, half // lane_blocks)
    assert lane_blocks * cuts == half
    cap = starts // n
    pieces = max(1, 16 // cap)
    return lanes, lane_blocks, cuts, cap, pieces


def kernel(
    n,
    x_ref,
    write_ref,
    read_ref,
    decay_ref,
    skip_ref,
    gain_ref,
    start_ref,
    value_w_ref,
    noise_hbm,
    act_hbm,
    dyn_hbm,
    act_in_hbm,
    out_hbm,
    post_hbm,
    values_ref,
    final_hbm,
    noise,
    act_w,
    dyn_w,
    act_in_w,
    out_w,
    meta_out,
    meta_in,
    end_out,
    end_in,
    carry_out,
    carry_in,
    cross_out,
    cross_in,
    local,
    entered,
    post,
    pick_out,
    pick_in,
    latent,
    load_sem,
    post_sem,
    meta_s,
    meta_r,
    end_s,
    end_r,
    carry_s,
    carry_r,
    cross_sem,
    pick_s,
    pick_r,
):
    rows, width = x_ref.shape
    heads = decay_ref.shape[0]
    state = write_ref.shape[0]
    starts = start_ref.shape[1]
    lanes, lane_blocks, cuts, cap, pieces = plan(n, rows, width, state, starts)
    head_width = width // heads
    half = n // 2
    depth = state // cuts
    slot_rows = pieces * cap
    piece_width = width // pieces
    me = lax.axis_index("seq")
    upper = me // half
    mine = lax.rem(me, half)
    base_of_half = upper * half

    def far_first(i):
        step = n // 2 + (i + 1) // 2 * (2 * lax.rem(i, 2) - 1)
        return lax.rem(me + step, n)

    loads = [
        pltpu.make_async_copy(src, dst, load_sem.at[i])
        for i, (src, dst) in enumerate(
            (
                (act_hbm, act_w),
                (dyn_hbm, dyn_w),
                (act_in_hbm, act_in_w),
                (out_hbm, out_w),
                (noise_hbm, noise),
            )
        )
    ]
    for load in loads:
        load.start()

    barrier = pltpu.get_barrier_semaphore()

    def greet(j, _):
        pl.semaphore_signal(
            barrier,
            inc=1,
            device_id={"seq": lax.rem(me + j, n)},
            device_id_type=pl.DeviceIdType.MESH,
        )
        return 0

    lax.fori_loop(1, n, greet, 0)

    def remote(src, dst, send, recv, peer, slot):
        return pltpu.make_async_remote_copy(
            src_ref=src,
            dst_ref=dst,
            send_sem=send.at[peer],
            recv_sem=recv.at[slot],
            device_id={"seq": peer},
            device_id_type=pl.DeviceIdType.MESH,
        )

    lower = iota((rows, rows), 0) >= iota((rows, rows), 1)
    running_t = jnp.dot(
        decay_ref[...],
        (iota((rows, rows), 0) <= iota((rows, rows), 1)).astype(F32),
        precision=lax.Precision.HIGHEST,
        preferred_element_type=F32,
    )
    running = running_t.T
    spread = (
        iota((2 * heads, width), 1) // head_width == lax.rem(iota((2 * heads, width), 0), heads)
    ).astype(BF16)

    def widen(v):
        high = v.astype(BF16).astype(F32)
        return dot(jnp.concatenate([high, v - high], axis=1).astype(BF16), spread)

    x_all = x_ref[...].astype(F32)
    tail = widen(jnp.exp(running[rows - 1 : rows] - running))
    end_state = dot(write_ref[...], (x_all * tail).astype(BF16))
    whole_decay = widen(jnp.exp(running[rows - 8 : rows]))[7:8]
    start_row = start_ref[...].astype(F32)
    for k in range(half):
        at = slice((k // cuts) * lanes, (k // cuts + 1) * lanes)
        end_out[k] = end_state[(k % cuts) * depth : (k % cuts + 1) * depth, at].astype(BF16)
    decay_rows = lanes // 128
    for k in range(n):
        first_lane = (k % half) // cuts * lanes
        meta_out[k, 0:1, :] = start_row
        for i in range(decay_rows):
            lane = first_lane + i * 128
            meta_out[k, 1 + i : 2 + i, :] = whole_decay[:, lane : lane + 128]

    pl.semaphore_wait(barrier, n - 1)

    def send_end(j, _):
        k = lax.rem(mine + j, half)
        pltpu.make_async_remote_copy(
            src_ref=end_out.at[k],
            dst_ref=end_in.at[mine],
            send_sem=end_s.at[k],
            recv_sem=end_r.at[mine],
            device_id={"seq": base_of_half + k},
            device_id_type=pl.DeviceIdType.MESH,
        ).start()
        return 0

    lax.fori_loop(1, half, send_end, 0)

    def send_meta(i, _):
        peer = far_first(i)
        remote(meta_out.at[peer], meta_in.at[me], meta_s, meta_r, peer, me).start()
        return 0

    lax.fori_loop(0, n - 1, send_meta, 0)
    meta_in[pl.ds(me, 1)] = meta_out[pl.ds(me, 1)]
    end_in[pl.ds(mine, 1)] = end_out[pl.ds(mine, 1)]

    eye_rows = (iota((rows, rows), 0) == iota((rows, rows), 1)).astype(BF16)
    read = dot_nt(eye_rows, read_ref[...]).astype(BF16)
    gram = dot(read, write_ref[...])
    skip = widen(jnp.broadcast_to(skip_ref[...], (8, heads)))[0:1]
    per_tile = 128 // head_width
    head_of = iota((rows, 128), 1) // head_width

    def local_tiles(tiles):
        for tile in tiles:
            at = slice(tile * 128, (tile + 1) * 128)
            x_tile = x_ref[:, at].astype(F32)
            total = x_tile * skip[:, at]
            for inner in range(per_tile):
                h = tile * per_tile + inner
                gap = running[:, h : h + 1] - running_t[h : h + 1, :]
                weight = (jnp.exp(jnp.where(lower, gap, -jnp.inf)) * gram).astype(BF16)
                one_head = jnp.where(head_of == inner, x_tile, 0.0).astype(BF16)
                total = total + dot(weight, one_head)
            local[:, at] = total

    tiles = width // 128
    local_tiles(range(tiles // 2))

    def wait_meta(d):
        remote(meta_out.at[0], meta_in.at[d], meta_s, meta_r, d, d).wait_recv()

    def ends_lap(j, _):
        k = lax.rem(mine + j, half)
        pltpu.make_async_remote_copy(
            src_ref=end_out.at[0],
            dst_ref=end_in.at[k],
            send_sem=end_s.at[k],
            recv_sem=end_r.at[k],
            device_id={"seq": base_of_half + k},
            device_id_type=pl.DeviceIdType.MESH,
        ).wait_recv()
        wait_meta(base_of_half + k)
        return 0

    lax.fori_loop(1, half, ends_lap, 0)

    across = pltpu.make_async_remote_copy(
        src_ref=cross_out,
        dst_ref=cross_in,
        send_sem=cross_sem.at[0],
        recv_sem=cross_sem.at[1],
        device_id={"seq": lax.rem(me + half, n)},
        device_id_type=pl.DeviceIdType.MESH,
    )

    @pl.when(upper == 0)
    def _():
        cross_in[...] = jnp.zeros_like(cross_in)

    @pl.when(upper == 1)
    def _():
        across.wait_recv()

    def fold(d, carry):
        carry_out[d] = carry.astype(BF16)
        decay = jnp.concatenate(
            [meta_in[base_of_half + d, 1 + i : 2 + i, :] for i in range(decay_rows)], axis=1
        )
        return carry * decay + end_in[d].astype(F32)

    cross_out[...] = lax.fori_loop(0, half, fold, cross_in[...].astype(F32)).astype(BF16)

    @pl.when(upper == 0)
    def _():
        across.start()

    def send_carry(j, _):
        k = lax.rem(mine + j, half)
        pltpu.make_async_remote_copy(
            src_ref=carry_out.at[k],
            dst_ref=carry_in.at[mine],
            send_sem=carry_s.at[k],
            recv_sem=carry_r.at[mine],
            device_id={"seq": base_of_half + k},
            device_id_type=pl.DeviceIdType.MESH,
        ).start()
        return 0

    lax.fori_loop(1, half, send_carry, 0)
    carry_in[pl.ds(mine, 1)] = carry_out[pl.ds(mine, 1)]

    local_tiles(range(tiles // 2, tiles))
    entered[...] = widen(jnp.exp(running))

    def metas_lap(j, _):
        wait_meta(lax.rem(base_of_half + half + j, n))
        return 0

    lax.fori_loop(0, half, metas_lap, 0)

    asked = meta_in[:, 0, :starts]
    base = (me * rows).astype(F32)
    hit = jnp.logical_and(asked >= base, asked < base + rows)
    up_to = (iota((starts, starts), 0) <= iota((starts, starts), 1)).astype(BF16)
    rank = dot(hit.astype(F32).astype(BF16), up_to)
    rank = jnp.where(hit, rank, 0.0).astype(BF16)
    offset = jnp.where(hit, asked - base, 0.0).astype(BF16)
    slots = n * slot_rows
    repeat = (iota((slots, n), 0) // slot_rows == iota((slots, n), 1)).astype(BF16)
    slot_at = iota((slots, starts), 0)
    chosen = dot(repeat, rank) == (slot_at % cap + 1).astype(F32)
    wanted = jnp.sum(jnp.where(chosen, dot(repeat, offset), 0.0), axis=1, keepdims=True)
    row_at = iota((slots, rows), 0)
    picks_row = wanted == iota((slots, rows), 1).astype(F32)
    picks = [
        jnp.where(jnp.logical_and(picks_row, (row_at // cap) % pieces == p), 1.0, 0.0).astype(BF16)
        for p in range(pieces)
    ]

    start_col = jnp.sum(
        jnp.where(iota((starts, starts), 0) == iota((starts, starts), 1), start_row, 0.0),
        axis=1,
        keepdims=True,
    )
    first = (iota((starts, n), 1) * rows).astype(F32)
    from_owner = jnp.logical_and(start_col >= first, start_col < first + rows)
    before = (iota((starts, starts), 0) >= iota((starts, starts), 1)).astype(BF16)
    count = dot(before, from_owner.astype(F32).astype(BF16))
    lands = jnp.sum(
        jnp.where(from_owner, count - 1.0 + (iota((starts, n), 1) * slot_rows).astype(F32), 0.0),
        axis=1,
        keepdims=True,
    )

    def carry_lap(j, _):
        k = lax.rem(mine + j, half)
        pltpu.make_async_remote_copy(
            src_ref=carry_out.at[0],
            dst_ref=carry_in.at[k],
            send_sem=carry_s.at[k],
            recv_sem=carry_r.at[k],
            device_id={"seq": base_of_half + k},
            device_id_type=pl.DeviceIdType.MESH,
        ).wait_recv()
        return 0

    lax.fori_loop(1, half, carry_lap, 0)
    same_head = jnp.where(
        iota((lanes, lanes), 0) // head_width == iota((lanes, lanes), 1) // head_width,
        1.0 / head_width,
        0.0,
    ).astype(BF16)
    for block in range(lane_blocks):
        at = slice(block * lanes, (block + 1) * lanes)
        carry = carry_in[block * cuts : (block + 1) * cuts].reshape(state, lanes)
        mixed = local[:, at] + dot(read, carry) * entered[:, at]
        square_mean = dot((mixed * mixed).astype(BF16), same_head)
        post[:, at] = (mixed * lax.rsqrt(square_mean + 1e-05) * gain_ref[:, at]).astype(BF16)
    picked = dot(picks[0], post[:, :piece_width])
    for p in range(1, pieces):
        picked = picked + dot(picks[p], post[:, p * piece_width : (p + 1) * piece_width])
    pick_out[...] = picked.astype(BF16).reshape(n, slot_rows, piece_width)

    def send_rows(i, _):
        peer = far_first(i)
        remote(pick_out.at[peer], pick_in.at[me], pick_s, pick_r, peer, me).start()
        return 0

    lax.fori_loop(0, n - 1, send_rows, 0)
    pick_in[pl.ds(me, 1)] = pick_out[pl.ds(me, 1)]
    post_copy = pltpu.make_async_copy(post, post_hbm, post_sem.at[0])
    post_copy.start()
    for load in loads:
        load.wait()

    def row_lap(j, _):
        peer = lax.rem(me + j, n)
        remote(pick_out.at[0], pick_in.at[peer], pick_s, pick_r, peer, peer).wait_recv()
        return 0

    lax.fori_loop(1, n, row_lap, 0)

    landed = pick_in[...].reshape(slots, piece_width)
    slot_of = iota((starts, slots), 1).astype(F32)
    for p in range(pieces):
        place = jnp.where(slot_of == lands + float(p * cap), 1.0, 0.0).astype(BF16)
        latent[:, p * piece_width : (p + 1) * piece_width] = dot(place, landed).astype(BF16)

    diagonal = iota((starts, starts), 0) == iota((starts, starts), 1)
    value_rows = value_w_ref[...].astype(F32)
    value_w = jnp.concatenate(
        [value_rows[i : i + 1] for i in range(value_rows.shape[0])], axis=1
    )
    for step in range(noise.shape[0]):
        wide = latent[...].astype(F32)
        normed = (
            wide * lax.rsqrt(jnp.mean(wide * wide, axis=-1, keepdims=True) + 1e-06)
        ).astype(BF16)
        action = jnp.tanh(dot(normed, act_w[...])).astype(BF16)
        inner = dot(normed, dyn_w[...]) + dot(action, act_in_w[...])
        hidden = (inner / (1.0 + jnp.exp(-inner)) + noise[step].astype(F32)).astype(BF16)
        value = jnp.sum(hidden.astype(F32) * value_w, axis=1, keepdims=True)
        values_ref[step : step + 1, :] = jnp.sum(
            jnp.where(diagonal, value, 0.0), axis=0, keepdims=True
        )
        latent[...] = (wide + dot(hidden, out_w[...])).astype(BF16)

    final_copy = pltpu.make_async_copy(latent, final_hbm, post_sem.at[1])
    final_copy.start()

    def sent(j, _):
        peer = lax.rem(me + j, n)
        remote(meta_out.at[0], meta_in.at[me], meta_s, meta_r, peer, me).wait_send()
        remote(pick_out.at[0], pick_in.at[me], pick_s, pick_r, peer, me).wait_send()

        return 0

    lax.fori_loop(1, n, sent, 0)

    def sent_in_half(j, _):
        k = lax.rem(mine + j, half)
        for src, dst, send, recv in (
            (end_out, end_in, end_s, end_r),
            (carry_out, carry_in, carry_s, carry_r),
        ):
            pltpu.make_async_remote_copy(
                src_ref=src.at[0],
                dst_ref=dst.at[mine],
                send_sem=send.at[k],
                recv_sem=recv.at[mine],
                device_id={"seq": base_of_half + k},
                device_id_type=pl.DeviceIdType.MESH,
            ).wait_send()
        return 0

    lax.fori_loop(1, half, sent_in_half, 0)

    @pl.when(upper == 0)
    def _():
        across.wait_send()

    post_copy.wait()
    final_copy.wait()


def hand_over(*refs):
    sem = refs[6]
    copies = [pltpu.make_async_copy(refs[i], refs[3 + i], sem.at[i]) for i in range(3)]
    for copy in copies:
        copy.start()
    for copy in copies:
        copy.wait()


def per_device(
    features,
    state_write,
    state_read,
    log_decay,
    skip_gain,
    post_gain,
    start_index,
    step_noise,
    act_weight,
    dyn_weight,
    act_in_weight,
    out_weight,
    value_weight,
):
    n = lax.axis_size("seq")
    rows, width = features.shape
    state = state_write.shape[1]
    starts = start_index.shape[0]
    lanes, lane_blocks, cuts, cap, pieces = plan(n, rows, width, state, starts)
    half, depth, slot_rows = n // 2, state // cuts, pieces * cap
    vmem = pl.BlockSpec(memory_space=pltpu.VMEM)
    hbm = pl.BlockSpec(memory_space=pl.ANY)
    sems = pltpu.SemaphoreType.DMA((n,))
    half_sems = pltpu.SemaphoreType.DMA((half,))
    flops = 2 * step_noise.shape[0] * starts * (dyn_weight.size + out_weight.size)
    results = pl.pallas_call(
        functools.partial(kernel, n),
        out_shape=(
            jax.ShapeDtypeStruct((rows, width), BF16),
            jax.ShapeDtypeStruct((step_noise.shape[0], starts), F32),
            jax.ShapeDtypeStruct((starts, width), BF16),
        ),
        in_specs=[vmem] * 8 + [hbm] * 5,
        out_specs=(hbm, vmem, hbm),
        scratch_shapes=[
            pltpu.VMEM(step_noise.shape, BF16),
            pltpu.VMEM(act_weight.shape, BF16),
            pltpu.VMEM(dyn_weight.shape, BF16),
            pltpu.VMEM(act_in_weight.shape, BF16),
            pltpu.VMEM(out_weight.shape, BF16),
            pltpu.VMEM((n, 8, 128), F32),
            pltpu.VMEM((n, 8, 128), F32),
            pltpu.VMEM((half, depth, lanes), BF16),
            pltpu.VMEM((half, depth, lanes), BF16),
            pltpu.VMEM((half, depth, lanes), BF16),
            pltpu.VMEM((half, depth, lanes), BF16),
            pltpu.VMEM((depth, lanes), BF16),
            pltpu.VMEM((depth, lanes), BF16),
            pltpu.VMEM((rows, width), F32),
            pltpu.VMEM((rows, width), F32),
            pltpu.VMEM((rows, width), BF16),
            pltpu.VMEM((n, slot_rows, width // pieces), BF16),
            pltpu.VMEM((n, slot_rows, width // pieces), BF16),
            pltpu.VMEM((starts, width), BF16),
            pltpu.SemaphoreType.DMA((5,)),
            pltpu.SemaphoreType.DMA((2,)),
            sems,
            sems,
            half_sems,
            half_sems,
            half_sems,
            half_sems,
            pltpu.SemaphoreType.DMA((2,)),
            sems,
            sems,
        ],
        compiler_params=pltpu.CompilerParams(
            collective_id=0, has_side_effects=True, vmem_limit_bytes=VMEM_LIMIT
        ),
        cost_estimate=pl.CostEstimate(
            flops=flops, bytes_accessed=12 * 1024 * 1024, transcendentals=1024 * 1024
        ),
    )(
        features,
        state_write.T,
        state_read.T,
        log_decay.T,
        skip_gain[None, :],
        post_gain[None, :],
        start_index[None, :],
        value_weight.reshape(-1, 128),
        step_noise,
        act_weight,
        dyn_weight,
        act_in_weight,
        out_weight,
    )
    return pl.pallas_call(
        hand_over,
        out_shape=tuple(jax.ShapeDtypeStruct(r.shape, r.dtype) for r in results),
        in_specs=[hbm] * 3,
        out_specs=(hbm, hbm, hbm),
        scratch_shapes=[pltpu.SemaphoreType.DMA((3,))],
        compiler_params=pltpu.CompilerParams(vmem_limit_bytes=VMEM_LIMIT),
    )(*results)


def solution(mesh):
    split = P(("groups", "seq"), None)
    placed = (
        split,
        split,
        split,
        split,
        P(),
        P(),
        P(("groups", "seq")),
        P(None, ("groups", "seq"), None),
        P(),
        P(),
        P(),
        P(),
        P(),
    )
    return jax.shard_map(
        per_device,
        mesh=mesh,
        in_specs=placed,
        out_specs=(split, P(None, ("groups", "seq")), split),
        check_vma=False,
    )
```

```python
import functools
import jax
import jax.numpy as jnp
from jax import lax
from jax.experimental import pallas as pl
from jax.experimental.pallas import tpu as pltpu
from jax.sharding import PartitionSpec as P

F32 = jnp.float32
BF16 = jnp.bfloat16
VMEM_LIMIT = 56 * 1024 * 1024


def dot(a, b):
    return jnp.dot(a, b, preferred_element_type=F32)


def dot_nt(a, b):
    return lax.dot_general(a, b, (((1,), (1,)), ((), ())), preferred_element_type=F32)


def iota(shape, dim):
    return lax.broadcasted_iota(jnp.int32, shape, dim)


def plan(n, rows, width, state, starts):
    half = n // 2
    lanes = max(128, width // half)
    lane_blocks = width // lanes
    cuts = min(state // 16, half // lane_blocks)
    assert lane_blocks * cuts == half
    cap = starts // n
    pieces = max(1, 16 // cap)
    return lanes, lane_blocks, cuts, cap, pieces


def kernel(
    n,
    x_ref,
    write_ref,
    read_ref,
    decay_ref,
    skip_ref,
    gain_ref,
    start_ref,
    value_w_ref,
    noise_hbm,
    act_hbm,
    dyn_hbm,
    act_in_hbm,
    out_hbm,
    post_hbm,
    values_ref,
    final_hbm,
    noise,
    act_w,
    dyn_w,
    act_in_w,
    out_w,
    meta_out,
    meta_in,
    end_out,
    end_in,
    carry_out,
    carry_in,
    cross_out,
    cross_in,
    local,
    entered,
    post,
    pick_out,
    pick_in,
    latent,
    load_sem,
    post_sem,
    meta_s,
    meta_r,
    end_s,
    end_r,
    carry_s,
    carry_r,
    cross_sem,
    pick_s,
    pick_r,
):
    rows, width = x_ref.shape
    heads = decay_ref.shape[0]
    state = write_ref.shape[0]
    starts = start_ref.shape[1]
    lanes, lane_blocks, cuts, cap, pieces = plan(n, rows, width, state, starts)
    head_width = width // heads
    half = n // 2
    depth = state // cuts
    slot_rows = pieces * cap
    piece_width = width // pieces
    me = lax.axis_index("seq")
    upper = me // half
    mine = lax.rem(me, half)
    base_of_half = upper * half

    def far_first(i):
        step = n // 2 + (i + 1) // 2 * (2 * lax.rem(i, 2) - 1)
        return lax.rem(me + step, n)

    loads = [
        pltpu.make_async_copy(src, dst, load_sem.at[i])
        for i, (src, dst) in enumerate(
            (
                (act_hbm, act_w),
                (dyn_hbm, dyn_w),
                (act_in_hbm, act_in_w),
                (out_hbm, out_w),
                (noise_hbm, noise),
            )
        )
    ]
    for load in loads:
        load.start()

    barrier = pltpu.get_barrier_semaphore()

    def greet(j, _):
        pl.semaphore_signal(
            barrier,
            inc=1,
            device_id={"seq": lax.rem(me + j, n)},
            device_id_type=pl.DeviceIdType.MESH,
        )
        return 0

    lax.fori_loop(1, n, greet, 0)

    def remote(src, dst, send, recv, peer, slot):
        return pltpu.make_async_remote_copy(
            src_ref=src,
            dst_ref=dst,
            send_sem=send.at[peer],
            recv_sem=recv.at[slot],
            device_id={"seq": peer},
            device_id_type=pl.DeviceIdType.MESH,
        )

    lower = iota((rows, rows), 0) >= iota((rows, rows), 1)
    running_t = jnp.dot(
        decay_ref[...],
        (iota((rows, rows), 0) <= iota((rows, rows), 1)).astype(F32),
        precision=lax.Precision.HIGHEST,
        preferred_element_type=F32,
    )
    running = running_t.T
    spread = (
        iota((2 * heads, width), 1) // head_width == lax.rem(iota((2 * heads, width), 0), heads)
    ).astype(BF16)

    def widen(v):
        high = v.astype(BF16).astype(F32)
        return dot(jnp.concatenate([high, v - high], axis=1).astype(BF16), spread)

    x_all = x_ref[...].astype(F32)
    tail = widen(jnp.exp(running[rows - 1 : rows] - running))
    end_state = dot(write_ref[...], (x_all * tail).astype(BF16))
    whole_decay = widen(jnp.exp(running[rows - 8 : rows]))[7:8]
    start_row = start_ref[...].astype(F32)
    for k in range(half):
        at = slice((k // cuts) * lanes, (k // cuts + 1) * lanes)
        end_out[k] = end_state[(k % cuts) * depth : (k % cuts + 1) * depth, at].astype(BF16)
    decay_rows = lanes // 128
    for k in range(n):
        first_lane = (k % half) // cuts * lanes
        meta_out[k, 0:1, :] = start_row
        for i in range(decay_rows):
            lane = first_lane + i * 128
            meta_out[k, 1 + i : 2 + i, :] = whole_decay[:, lane : lane + 128]

    pl.semaphore_wait(barrier, n - 1)

    def send_end(j, _):
        k = lax.rem(mine + j, half)
        pltpu.make_async_remote_copy(
            src_ref=end_out.at[k],
            dst_ref=end_in.at[mine],
            send_sem=end_s.at[k],
            recv_sem=end_r.at[mine],
            device_id={"seq": base_of_half + k},
            device_id_type=pl.DeviceIdType.MESH,
        ).start()
        return 0

    lax.fori_loop(1, half, send_end, 0)

    def send_meta(i, _):
        peer = far_first(i)
        remote(meta_out.at[peer], meta_in.at[me], meta_s, meta_r, peer, me).start()
        return 0

    lax.fori_loop(0, n - 1, send_meta, 0)
    meta_in[pl.ds(me, 1)] = meta_out[pl.ds(me, 1)]
    end_in[pl.ds(mine, 1)] = end_out[pl.ds(mine, 1)]

    eye_rows = (iota((rows, rows), 0) == iota((rows, rows), 1)).astype(BF16)
    read = dot_nt(eye_rows, read_ref[...]).astype(BF16)
    gram = dot(read, write_ref[...])
    skip = widen(jnp.broadcast_to(skip_ref[...], (8, heads)))[0:1]
    per_tile = 128 // head_width
    head_of = iota((rows, 128), 1) // head_width

    def local_tiles(tiles):
        for tile in tiles:
            at = slice(tile * 128, (tile + 1) * 128)
            x_tile = x_ref[:, at].astype(F32)
            total = x_tile * skip[:, at]
            for inner in range(per_tile):
                h = tile * per_tile + inner
                gap = running[:, h : h + 1] - running_t[h : h + 1, :]
                weight = (jnp.exp(jnp.where(lower, gap, -jnp.inf)) * gram).astype(BF16)
                one_head = jnp.where(head_of == inner, x_tile, 0.0).astype(BF16)
                total = total + dot(weight, one_head)
            local[:, at] = total

    tiles = width // 128
    local_tiles(range(tiles // 2))

    def wait_meta(d):
        remote(meta_out.at[0], meta_in.at[d], meta_s, meta_r, d, d).wait_recv()

    def ends_lap(j, _):
        k = lax.rem(mine + j, half)
        pltpu.make_async_remote_copy(
            src_ref=end_out.at[0],
            dst_ref=end_in.at[k],
            send_sem=end_s.at[k],
            recv_sem=end_r.at[k],
            device_id={"seq": base_of_half + k},
            device_id_type=pl.DeviceIdType.MESH,
        ).wait_recv()
        wait_meta(base_of_half + k)
        return 0

    lax.fori_loop(1, half, ends_lap, 0)

    across = pltpu.make_async_remote_copy(
        src_ref=cross_out,
        dst_ref=cross_in,
        send_sem=cross_sem.at[0],
        recv_sem=cross_sem.at[1],
        device_id={"seq": lax.rem(me + half, n)},
        device_id_type=pl.DeviceIdType.MESH,
    )

    @pl.when(upper == 0)
    def _():
        cross_in[...] = jnp.zeros_like(cross_in)

    @pl.when(upper == 1)
    def _():
        across.wait_recv()

    def fold(d, carry):
        carry_out[d] = carry.astype(BF16)
        decay = jnp.concatenate(
            [meta_in[base_of_half + d, 1 + i : 2 + i, :] for i in range(decay_rows)], axis=1
        )
        return carry * decay + end_in[d].astype(F32)

    cross_out[...] = lax.fori_loop(0, half, fold, cross_in[...].astype(F32)).astype(BF16)

    @pl.when(upper == 0)
    def _():
        across.start()

    def send_carry(j, _):
        k = lax.rem(mine + j, half)
        pltpu.make_async_remote_copy(
            src_ref=carry_out.at[k],
            dst_ref=carry_in.at[mine],
            send_sem=carry_s.at[k],
            recv_sem=carry_r.at[mine],
            device_id={"seq": base_of_half + k},
            device_id_type=pl.DeviceIdType.MESH,
        ).start()
        return 0

    lax.fori_loop(1, half, send_carry, 0)
    carry_in[pl.ds(mine, 1)] = carry_out[pl.ds(mine, 1)]

    local_tiles(range(tiles // 2, tiles))
    entered[...] = widen(jnp.exp(running))

    def metas_lap(j, _):
        wait_meta(lax.rem(base_of_half + half + j, n))
        return 0

    lax.fori_loop(0, half, metas_lap, 0)

    asked = meta_in[:, 0, :starts]
    base = (me * rows).astype(F32)
    hit = jnp.logical_and(asked >= base, asked < base + rows)
    up_to = (iota((starts, starts), 0) <= iota((starts, starts), 1)).astype(BF16)
    rank = dot(hit.astype(F32).astype(BF16), up_to)
    rank = jnp.where(hit, rank, 0.0).astype(BF16)
    offset = jnp.where(hit, asked - base, 0.0).astype(BF16)
    slots = n * slot_rows
    repeat = (iota((slots, n), 0) // slot_rows == iota((slots, n), 1)).astype(BF16)
    slot_at = iota((slots, starts), 0)
    chosen = dot(repeat, rank) == (slot_at % cap + 1).astype(F32)
    wanted = jnp.sum(jnp.where(chosen, dot(repeat, offset), 0.0), axis=1, keepdims=True)
    row_at = iota((slots, rows), 0)
    picks_row = wanted == iota((slots, rows), 1).astype(F32)
    picks = [
        jnp.where(jnp.logical_and(picks_row, (row_at // cap) % pieces == p), 1.0, 0.0).astype(BF16)
        for p in range(pieces)
    ]

    start_col = jnp.sum(
        jnp.where(iota((starts, starts), 0) == iota((starts, starts), 1), start_row, 0.0),
        axis=1,
        keepdims=True,
    )
    first = (iota((starts, n), 1) * rows).astype(F32)
    from_owner = jnp.logical_and(start_col >= first, start_col < first + rows)
    before = (iota((starts, starts), 0) >= iota((starts, starts), 1)).astype(BF16)
    count = dot(before, from_owner.astype(F32).astype(BF16))
    lands = jnp.sum(
        jnp.where(from_owner, count - 1.0 + (iota((starts, n), 1) * slot_rows).astype(F32), 0.0),
        axis=1,
        keepdims=True,
    )

    def carry_lap(j, _):
        k = lax.rem(mine + j, half)
        pltpu.make_async_remote_copy(
            src_ref=carry_out.at[0],
            dst_ref=carry_in.at[k],
            send_sem=carry_s.at[k],
            recv_sem=carry_r.at[k],
            device_id={"seq": base_of_half + k},
            device_id_type=pl.DeviceIdType.MESH,
        ).wait_recv()
        return 0

    lax.fori_loop(1, half, carry_lap, 0)
    same_head = jnp.where(
        iota((lanes, lanes), 0) // head_width == iota((lanes, lanes), 1) // head_width,
        1.0 / head_width,
        0.0,
    ).astype(BF16)
    for block in range(lane_blocks):
        at = slice(block * lanes, (block + 1) * lanes)
        carry = carry_in[block * cuts : (block + 1) * cuts].reshape(state, lanes)
        mixed = local[:, at] + dot(read, carry) * entered[:, at]
        square_mean = dot((mixed * mixed).astype(BF16), same_head)
        post[:, at] = (mixed * lax.rsqrt(square_mean + 1e-05) * gain_ref[:, at]).astype(BF16)
    picked = dot(picks[0], post[:, :piece_width])
    for p in range(1, pieces):
        picked = picked + dot(picks[p], post[:, p * piece_width : (p + 1) * piece_width])
    pick_out[...] = picked.astype(BF16).reshape(n, slot_rows, piece_width)

    def send_rows(i, _):
        peer = far_first(i)
        remote(pick_out.at[peer], pick_in.at[me], pick_s, pick_r, peer, me).start()
        return 0

    lax.fori_loop(0, n - 1, send_rows, 0)
    pick_in[pl.ds(me, 1)] = pick_out[pl.ds(me, 1)]
    post_copy = pltpu.make_async_copy(post, post_hbm, post_sem.at[0])
    post_copy.start()
    for load in loads:
        load.wait()

    def row_lap(j, _):
        peer = lax.rem(me + j, n)
        remote(pick_out.at[0], pick_in.at[peer], pick_s, pick_r, peer, peer).wait_recv()
        return 0

    lax.fori_loop(1, n, row_lap, 0)

    landed = pick_in[...].reshape(slots, piece_width)
    slot_of = iota((starts, slots), 1).astype(F32)
    for p in range(pieces):
        place = jnp.where(slot_of == lands + float(p * cap), 1.0, 0.0).astype(BF16)
        latent[:, p * piece_width : (p + 1) * piece_width] = dot(place, landed).astype(BF16)

    diagonal = iota((starts, starts), 0) == iota((starts, starts), 1)
    value_rows = value_w_ref[...].astype(F32)
    value_w = jnp.concatenate(
        [value_rows[i : i + 1] for i in range(value_rows.shape[0])], axis=1
    )
    for step in range(noise.shape[0]):
        wide = latent[...].astype(F32)
        normed = (
            wide * lax.rsqrt(jnp.mean(wide * wide, axis=-1, keepdims=True) + 1e-06)
        ).astype(BF16)
        action = jnp.tanh(dot(normed, act_w[...])).astype(BF16)
        inner = dot(normed, dyn_w[...]) + dot(action, act_in_w[...])
        hidden = (inner / (1.0 + jnp.exp(-inner)) + noise[step].astype(F32)).astype(BF16)
        value = jnp.sum(hidden.astype(F32) * value_w, axis=1, keepdims=True)
        values_ref[step : step + 1, :] = jnp.sum(
            jnp.where(diagonal, value, 0.0), axis=0, keepdims=True
        )
        latent[...] = (wide + dot(hidden, out_w[...])).astype(BF16)

    final_copy = pltpu.make_async_copy(latent, final_hbm, post_sem.at[1])
    final_copy.start()

    def sent(j, _):
        peer = lax.rem(me + j, n)
        remote(meta_out.at[0], meta_in.at[me], meta_s, meta_r, peer, me).wait_send()
        remote(pick_out.at[0], pick_in.at[me], pick_s, pick_r, peer, me).wait_send()

        return 0

    lax.fori_loop(1, n, sent, 0)

    def sent_in_half(j, _):
        k = lax.rem(mine + j, half)
        for src, dst, send, recv in (
            (end_out, end_in, end_s, end_r),
            (carry_out, carry_in, carry_s, carry_r),
        ):
            pltpu.make_async_remote_copy(
                src_ref=src.at[0],
                dst_ref=dst.at[mine],
                send_sem=send.at[k],
                recv_sem=recv.at[mine],
                device_id={"seq": base_of_half + k},
                device_id_type=pl.DeviceIdType.MESH,
            ).wait_send()
        return 0

    lax.fori_loop(1, half, sent_in_half, 0)

    @pl.when(upper == 0)
    def _():
        across.wait_send()

    post_copy.wait()
    final_copy.wait()


def hand_over(*refs):
    sem = refs[6]
    copies = [pltpu.make_async_copy(refs[i], refs[3 + i], sem.at[i]) for i in range(3)]
    for copy in copies:
        copy.start()
    for copy in copies:
        copy.wait()


def per_device(
    features,
    state_write,
    state_read,
    log_decay,
    skip_gain,
    post_gain,
    start_index,
    step_noise,
    act_weight,
    dyn_weight,
    act_in_weight,
    out_weight,
    value_weight,
):
    n = lax.axis_size("seq")
    rows, width = features.shape
    state = state_write.shape[1]
    starts = start_index.shape[0]
    lanes, lane_blocks, cuts, cap, pieces = plan(n, rows, width, state, starts)
    half, depth, slot_rows = n // 2, state // cuts, pieces * cap
    vmem = pl.BlockSpec(memory_space=pltpu.VMEM)
    hbm = pl.BlockSpec(memory_space=pl.ANY)
    sems = pltpu.SemaphoreType.DMA((n,))
    half_sems = pltpu.SemaphoreType.DMA((half,))
    flops = 2 * step_noise.shape[0] * starts * (dyn_weight.size + out_weight.size)
    results = pl.pallas_call(
        functools.partial(kernel, n),
        out_shape=(
            jax.ShapeDtypeStruct((rows, width), BF16),
            jax.ShapeDtypeStruct((step_noise.shape[0], starts), F32),
            jax.ShapeDtypeStruct((starts, width), BF16),
        ),
        in_specs=[vmem] * 8 + [hbm] * 5,
        out_specs=(hbm, vmem, hbm),
        scratch_shapes=[
            pltpu.VMEM(step_noise.shape, BF16),
            pltpu.VMEM(act_weight.shape, BF16),
            pltpu.VMEM(dyn_weight.shape, BF16),
            pltpu.VMEM(act_in_weight.shape, BF16),
            pltpu.VMEM(out_weight.shape, BF16),
            pltpu.VMEM((n, 8, 128), F32),
            pltpu.VMEM((n, 8, 128), F32),
            pltpu.VMEM((half, depth, lanes), BF16),
            pltpu.VMEM((half, depth, lanes), BF16),
            pltpu.VMEM((half, depth, lanes), BF16),
            pltpu.VMEM((half, depth, lanes), BF16),
            pltpu.VMEM((depth, lanes), BF16),
            pltpu.VMEM((depth, lanes), BF16),
            pltpu.VMEM((rows, width), F32),
            pltpu.VMEM((rows, width), F32),
            pltpu.VMEM((rows, width), BF16),
            pltpu.VMEM((n, slot_rows, width // pieces), BF16),
            pltpu.VMEM((n, slot_rows, width // pieces), BF16),
            pltpu.VMEM((starts, width), BF16),
            pltpu.SemaphoreType.DMA((5,)),
            pltpu.SemaphoreType.DMA((2,)),
            sems,
            sems,
            half_sems,
            half_sems,
            half_sems,
            half_sems,
            pltpu.SemaphoreType.DMA((2,)),
            sems,
            sems,
        ],
        compiler_params=pltpu.CompilerParams(
            collective_id=0, has_side_effects=True, vmem_limit_bytes=VMEM_LIMIT
        ),
        cost_estimate=pl.CostEstimate(
            flops=flops, bytes_accessed=12 * 1024 * 1024, transcendentals=1024 * 1024
        ),
    )(
        features,
        state_write.T,
        state_read.T,
        log_decay.T,
        skip_gain[None, :],
        post_gain[None, :],
        start_index[None, :],
        value_weight.reshape(-1, 128),
        step_noise,
        act_weight,
        dyn_weight,
        act_in_weight,
        out_weight,
    )
    return pl.pallas_call(
        hand_over,
        out_shape=tuple(jax.ShapeDtypeStruct(r.shape, r.dtype) for r in results),
        in_specs=[vmem] * 3,
        out_specs=(hbm, hbm, hbm),
        scratch_shapes=[pltpu.SemaphoreType.DMA((3,))],
    )(*results)


def solution(mesh):
    split = P(("groups", "seq"), None)
    placed = (
        split,
        split,
        split,
        split,
        P(),
        P(),
        P(("groups", "seq")),
        P(None, ("groups", "seq"), None),
        P(),
        P(),
        P(),
        P(),
        P(),
    )
    return jax.shard_map(
        per_device,
        mesh=mesh,
        in_specs=placed,
        out_specs=(split, P(None, ("groups", "seq")), split),
        check_vma=False,
    )
```

```python
import functools
import jax
import jax.numpy as jnp
from jax import lax
from jax.experimental import pallas as pl
from jax.experimental.pallas import tpu as pltpu
from jax.sharding import PartitionSpec as P

F32 = jnp.float32
BF16 = jnp.bfloat16
VMEM_LIMIT = 56 * 1024 * 1024


def dot(a, b):
    return jnp.dot(a, b, preferred_element_type=F32)


def dot_nt(a, b):
    return lax.dot_general(a, b, (((1,), (1,)), ((), ())), preferred_element_type=F32)


def iota(shape, dim):
    return lax.broadcasted_iota(jnp.int32, shape, dim)


def plan(n, rows, width, state, starts):
    half = n // 2
    lanes = max(128, width // half)
    lane_blocks = width // lanes
    cuts = min(state // 16, half // lane_blocks)
    assert lane_blocks * cuts == half
    cap = starts // n
    pieces = max(1, 16 // cap)
    parts = 2 if width // 2 // pieces >= 128 and lane_blocks % 2 == 0 else 1
    return lanes, lane_blocks, cuts, cap, pieces, parts


def kernel(
    n,
    x_ref,
    write_ref,
    read_ref,
    decay_ref,
    skip_ref,
    gain_ref,
    start_ref,
    value_w_ref,
    noise_hbm,
    act_hbm,
    dyn_hbm,
    act_in_hbm,
    out_hbm,
    post,
    values_ref,
    latent,
    noise,
    act_w,
    dyn_w,
    act_in_w,
    out_w,
    meta_out,
    meta_in,
    end_out,
    end_in,
    carry_out,
    carry_in,
    cross_out,
    cross_in,
    local,
    entered,
    pick_out,
    pick_in,
    load_sem,
    meta_s,
    meta_r,
    end_s,
    end_r,
    carry_s,
    carry_r,
    cross_sem,
    pick_s,
    pick_r,
):
    rows, width = x_ref.shape
    heads = decay_ref.shape[0]
    state = write_ref.shape[0]
    starts = start_ref.shape[1]
    lanes, lane_blocks, cuts, cap, pieces, parts = plan(n, rows, width, state, starts)
    head_width = width // heads
    half = n // 2
    depth = state // cuts
    slot_rows = pieces * cap
    part_width = width // parts
    piece_width = part_width // pieces
    me = lax.axis_index("seq")
    upper = me // half
    mine = lax.rem(me, half)
    base_of_half = upper * half

    def far_first(i):
        step = n // 2 + (i + 1) // 2 * (2 * lax.rem(i, 2) - 1)
        return lax.rem(me + step, n)

    loads = [
        pltpu.make_async_copy(src, dst, load_sem.at[i])
        for i, (src, dst) in enumerate(
            (
                (act_hbm, act_w),
                (dyn_hbm, dyn_w),
                (act_in_hbm, act_in_w),
                (out_hbm, out_w),
                (noise_hbm, noise),
            )
        )
    ]
    for load in loads:
        load.start()

    barrier = pltpu.get_barrier_semaphore()

    def greet(j, _):
        pl.semaphore_signal(
            barrier,
            inc=1,
            device_id={"seq": lax.rem(me + j, n)},
            device_id_type=pl.DeviceIdType.MESH,
        )
        return 0

    lax.fori_loop(1, n, greet, 0)

    def remote(src, dst, send, recv, peer, slot):
        return pltpu.make_async_remote_copy(
            src_ref=src,
            dst_ref=dst,
            send_sem=send.at[peer],
            recv_sem=recv.at[slot],
            device_id={"seq": peer},
            device_id_type=pl.DeviceIdType.MESH,
        )

    lower = iota((rows, rows), 0) >= iota((rows, rows), 1)
    running_t = jnp.dot(
        decay_ref[...],
        (iota((rows, rows), 0) <= iota((rows, rows), 1)).astype(F32),
        precision=lax.Precision.HIGHEST,
        preferred_element_type=F32,
    )
    running = running_t.T
    spread = (
        iota((2 * heads, width), 1) // head_width == lax.rem(iota((2 * heads, width), 0), heads)
    ).astype(BF16)

    def widen(v):
        high = v.astype(BF16).astype(F32)
        return dot(jnp.concatenate([high, v - high], axis=1).astype(BF16), spread)

    x_all = x_ref[...].astype(F32)
    tail = widen(jnp.exp(running[rows - 1 : rows] - running))
    end_state = dot(write_ref[...], (x_all * tail).astype(BF16))
    whole_decay = widen(jnp.exp(running[rows - 8 : rows]))[7:8]
    start_row = start_ref[...].astype(F32)
    for k in range(half):
        at = slice((k // cuts) * lanes, (k // cuts + 1) * lanes)
        end_out[k] = end_state[(k % cuts) * depth : (k % cuts + 1) * depth, at].astype(BF16)
    decay_rows = lanes // 128
    for k in range(n):
        first_lane = (k % half) // cuts * lanes
        meta_out[k, 0:1, :] = start_row
        for i in range(decay_rows):
            lane = first_lane + i * 128
            meta_out[k, 1 + i : 2 + i, :] = whole_decay[:, lane : lane + 128]

    pl.semaphore_wait(barrier, n - 1)

    def send_end(j, _):
        k = lax.rem(mine + j, half)
        pltpu.make_async_remote_copy(
            src_ref=end_out.at[k],
            dst_ref=end_in.at[mine],
            send_sem=end_s.at[k],
            recv_sem=end_r.at[mine],
            device_id={"seq": base_of_half + k},
            device_id_type=pl.DeviceIdType.MESH,
        ).start()
        return 0

    lax.fori_loop(1, half, send_end, 0)

    def send_meta(i, _):
        peer = far_first(i)
        remote(meta_out.at[peer], meta_in.at[me], meta_s, meta_r, peer, me).start()
        return 0

    lax.fori_loop(0, n - 1, send_meta, 0)
    meta_in[pl.ds(me, 1)] = meta_out[pl.ds(me, 1)]
    end_in[pl.ds(mine, 1)] = end_out[pl.ds(mine, 1)]

    eye_rows = (iota((rows, rows), 0) == iota((rows, rows), 1)).astype(BF16)
    read = dot_nt(eye_rows, read_ref[...]).astype(BF16)
    gram = dot(read, write_ref[...])
    skip = widen(jnp.broadcast_to(skip_ref[...], (8, heads)))[0:1]
    per_tile = 128 // head_width
    head_of = iota((rows, 128), 1) // head_width

    def local_tiles(tiles):
        for tile in tiles:
            at = slice(tile * 128, (tile + 1) * 128)
            x_tile = x_ref[:, at].astype(F32)
            total = x_tile * skip[:, at]
            for inner in range(per_tile):
                h = tile * per_tile + inner
                gap = running[:, h : h + 1] - running_t[h : h + 1, :]
                weight = (jnp.exp(jnp.where(lower, gap, -jnp.inf)) * gram).astype(BF16)
                one_head = jnp.where(head_of == inner, x_tile, 0.0).astype(BF16)
                total = total + dot(weight, one_head)
            local[:, at] = total

    tiles = width // 128
    local_tiles(range(tiles // 2))

    def wait_meta(d):
        remote(meta_out.at[0], meta_in.at[d], meta_s, meta_r, d, d).wait_recv()

    def ends_lap(j, _):
        k = lax.rem(mine + j, half)
        pltpu.make_async_remote_copy(
            src_ref=end_out.at[0],
            dst_ref=end_in.at[k],
            send_sem=end_s.at[k],
            recv_sem=end_r.at[k],
            device_id={"seq": base_of_half + k},
            device_id_type=pl.DeviceIdType.MESH,
        ).wait_recv()
        wait_meta(base_of_half + k)
        return 0

    lax.fori_loop(1, half, ends_lap, 0)

    across = pltpu.make_async_remote_copy(
        src_ref=cross_out,
        dst_ref=cross_in,
        send_sem=cross_sem.at[0],
        recv_sem=cross_sem.at[1],
        device_id={"seq": lax.rem(me + half, n)},
        device_id_type=pl.DeviceIdType.MESH,
    )

    @pl.when(upper == 0)
    def _():
        cross_in[...] = jnp.zeros_like(cross_in)

    @pl.when(upper == 1)
    def _():
        across.wait_recv()

    def fold(d, carry):
        carry_out[d] = carry.astype(BF16)
        decay = jnp.concatenate(
            [meta_in[base_of_half + d, 1 + i : 2 + i, :] for i in range(decay_rows)], axis=1
        )
        return carry * decay + end_in[d].astype(F32)

    cross_out[...] = lax.fori_loop(0, half, fold, cross_in[...].astype(F32)).astype(BF16)

    @pl.when(upper == 0)
    def _():
        across.start()

    def send_carry(j, _):
        k = lax.rem(mine + j, half)
        pltpu.make_async_remote_copy(
            src_ref=carry_out.at[k],
            dst_ref=carry_in.at[mine],
            send_sem=carry_s.at[k],
            recv_sem=carry_r.at[mine],
            device_id={"seq": base_of_half + k},
            device_id_type=pl.DeviceIdType.MESH,
        ).start()
        return 0

    lax.fori_loop(1, half, send_carry, 0)
    carry_in[pl.ds(mine, 1)] = carry_out[pl.ds(mine, 1)]

    local_tiles(range(tiles // 2, tiles))
    entered[...] = widen(jnp.exp(running))

    def metas_lap(j, _):
        wait_meta(lax.rem(base_of_half + half + j, n))
        return 0

    lax.fori_loop(0, half, metas_lap, 0)

    asked = meta_in[:, 0, :starts]
    base = (me * rows).astype(F32)
    hit = jnp.logical_and(asked >= base, asked < base + rows)
    up_to = (iota((starts, starts), 0) <= iota((starts, starts), 1)).astype(BF16)
    rank = dot(hit.astype(F32).astype(BF16), up_to)
    rank = jnp.where(hit, rank, 0.0).astype(BF16)
    offset = jnp.where(hit, asked - base, 0.0).astype(BF16)
    slots = n * slot_rows
    repeat = (iota((slots, n), 0) // slot_rows == iota((slots, n), 1)).astype(BF16)
    slot_at = iota((slots, starts), 0)
    chosen = dot(repeat, rank) == (slot_at % cap + 1).astype(F32)
    wanted = jnp.sum(jnp.where(chosen, dot(repeat, offset), 0.0), axis=1, keepdims=True)
    row_at = iota((slots, rows), 0)
    picks_row = wanted == iota((slots, rows), 1).astype(F32)
    picks = [
        jnp.where(jnp.logical_and(picks_row, (row_at // cap) % pieces == p), 1.0, 0.0).astype(BF16)
        for p in range(pieces)
    ]

    start_col = jnp.sum(
        jnp.where(iota((starts, starts), 0) == iota((starts, starts), 1), start_row, 0.0),
        axis=1,
        keepdims=True,
    )
    first = (iota((starts, n), 1) * rows).astype(F32)
    from_owner = jnp.logical_and(start_col >= first, start_col < first + rows)
    before = (iota((starts, starts), 0) >= iota((starts, starts), 1)).astype(BF16)
    count = dot(before, from_owner.astype(F32).astype(BF16))
    lands = jnp.sum(
        jnp.where(from_owner, count - 1.0 + (iota((starts, n), 1) * slot_rows).astype(F32), 0.0),
        axis=1,
        keepdims=True,
    )

    def carry_lap(k, _):
        @pl.when(k != mine)
        def _():
            pltpu.make_async_remote_copy(
                src_ref=carry_out.at[0],
                dst_ref=carry_in.at[k],
                send_sem=carry_s.at[k],
                recv_sem=carry_r.at[k],
                device_id={"seq": base_of_half + k},
                device_id_type=pl.DeviceIdType.MESH,
            ).wait_recv()

        return 0

    same_head = jnp.where(
        iota((lanes, lanes), 0) // head_width == iota((lanes, lanes), 1) // head_width,
        1.0 / head_width,
        0.0,
    ).astype(BF16)
    for part in range(parts):
        lax.fori_loop(part * half // parts, (part + 1) * half // parts, carry_lap, 0)
        for block in range(part * lane_blocks // parts, (part + 1) * lane_blocks // parts):
            at = slice(block * lanes, (block + 1) * lanes)
            carry = carry_in[block * cuts : (block + 1) * cuts].reshape(state, lanes)
            mixed = local[:, at] + dot(read, carry) * entered[:, at]
            square_mean = dot((mixed * mixed).astype(BF16), same_head)
            post[:, at] = (mixed * lax.rsqrt(square_mean + 1e-05) * gain_ref[:, at]).astype(BF16)
        picked = 0.0
        for p in range(pieces):
            lane = part * part_width + p * piece_width
            picked = picked + dot(picks[p], post[:, lane : lane + piece_width])
        pick_out[part] = picked.astype(BF16).reshape(n, slot_rows, piece_width)

        def send_rows(i, _):
            peer = far_first(i)
            remote(
                pick_out.at[part, peer],
                pick_in.at[part, me],
                pick_s.at[part],
                pick_r.at[part],
                peer,
                me,
            ).start()
            return 0

        lax.fori_loop(0, n - 1, send_rows, 0)
        pick_in[part, pl.ds(me, 1)] = pick_out[part, pl.ds(me, 1)]
    for load in loads:
        load.wait()

    slot_of = iota((starts, slots), 1).astype(F32)
    act_sum, dyn_sum = 0.0, 0.0
    for part in range(parts):

        def row_lap(j, _):
            peer = lax.rem(me + j, n)
            remote(
                pick_out.at[part, 0],
                pick_in.at[part, peer],
                pick_s.at[part],
                pick_r.at[part],
                peer,
                peer,
            ).wait_recv()
            return 0

        lax.fori_loop(1, n, row_lap, 0)
        landed = pick_in[part].reshape(slots, piece_width)
        for p in range(pieces):
            place = jnp.where(slot_of == lands + float(p * cap), 1.0, 0.0).astype(BF16)
            lane = part * part_width + p * piece_width
            latent[:, lane : lane + piece_width] = dot(place, landed).astype(BF16)
        at = slice(part * part_width, (part + 1) * part_width)
        act_sum = act_sum + dot(latent[:, at], act_w[at, :])
        dyn_sum = dyn_sum + dot(latent[:, at], dyn_w[at, :])

    diagonal = iota((starts, starts), 0) == iota((starts, starts), 1)
    value_rows = value_w_ref[...].astype(F32)
    value_w = jnp.concatenate(
        [value_rows[i : i + 1] for i in range(value_rows.shape[0])], axis=1
    )
    for step in range(noise.shape[0]):
        wide = latent[...].astype(F32)
        scale = lax.rsqrt(jnp.mean(wide * wide, axis=-1, keepdims=True) + 1e-06)
        if step > 0:
            act_sum = dot(latent[...], act_w[...])
            dyn_sum = dot(latent[...], dyn_w[...])
        action = jnp.tanh(act_sum * scale).astype(BF16)
        inner = dyn_sum * scale + dot(action, act_in_w[...])
        hidden = (inner / (1.0 + jnp.exp(-inner)) + noise[step].astype(F32)).astype(BF16)
        value = jnp.sum(hidden.astype(F32) * value_w, axis=1, keepdims=True)
        values_ref[step : step + 1, :] = jnp.sum(
            jnp.where(diagonal, value, 0.0), axis=0, keepdims=True
        )
        latent[...] = (wide + dot(hidden, out_w[...])).astype(BF16)

    def sent(j, _):
        peer = lax.rem(me + j, n)
        remote(meta_out.at[0], meta_in.at[me], meta_s, meta_r, peer, me).wait_send()
        for part in range(parts):
            remote(
                pick_out.at[part, 0],
                pick_in.at[part, me],
                pick_s.at[part],
                pick_r.at[part],
                peer,
                me,
            ).wait_send()

        return 0

    lax.fori_loop(1, n, sent, 0)

    def sent_in_half(j, _):
        k = lax.rem(mine + j, half)
        for src, dst, send, recv in (
            (end_out, end_in, end_s, end_r),
            (carry_out, carry_in, carry_s, carry_r),
        ):
            pltpu.make_async_remote_copy(
                src_ref=src.at[0],
                dst_ref=dst.at[mine],
                send_sem=send.at[k],
                recv_sem=recv.at[mine],
                device_id={"seq": base_of_half + k},
                device_id_type=pl.DeviceIdType.MESH,
            ).wait_send()
        return 0

    lax.fori_loop(1, half, sent_in_half, 0)

    @pl.when(upper == 0)
    def _():
        across.wait_send()


def hand_over(*refs):
    sem = refs[6]
    copies = [pltpu.make_async_copy(refs[i], refs[3 + i], sem.at[i]) for i in range(3)]
    for copy in copies:
        copy.start()
    for copy in copies:
        copy.wait()


def per_device(
    features,
    state_write,
    state_read,
    log_decay,
    skip_gain,
    post_gain,
    start_index,
    step_noise,
    act_weight,
    dyn_weight,
    act_in_weight,
    out_weight,
    value_weight,
):
    n = lax.axis_size("seq")
    rows, width = features.shape
    state = state_write.shape[1]
    starts = start_index.shape[0]
    lanes, lane_blocks, cuts, cap, pieces, parts = plan(n, rows, width, state, starts)
    half, depth, slot_rows = n // 2, state // cuts, pieces * cap
    vmem = pl.BlockSpec(memory_space=pltpu.VMEM)
    hbm = pl.BlockSpec(memory_space=pl.ANY)
    sems = pltpu.SemaphoreType.DMA((n,))
    half_sems = pltpu.SemaphoreType.DMA((half,))
    flops = 2 * step_noise.shape[0] * starts * (dyn_weight.size + out_weight.size)
    results = pl.pallas_call(
        functools.partial(kernel, n),
        out_shape=(
            pltpu.VMEM((rows, width), BF16),
            pltpu.VMEM((step_noise.shape[0], starts), F32),
            pltpu.VMEM((starts, width), BF16),
        ),
        in_specs=[vmem] * 8 + [hbm] * 5,
        out_specs=(vmem, vmem, vmem),
        scratch_shapes=[
            pltpu.VMEM(step_noise.shape, BF16),
            pltpu.VMEM(act_weight.shape, BF16),
            pltpu.VMEM(dyn_weight.shape, BF16),
            pltpu.VMEM(act_in_weight.shape, BF16),
            pltpu.VMEM(out_weight.shape, BF16),
            pltpu.VMEM((n, 8, 128), F32),
            pltpu.VMEM((n, 8, 128), F32),
            pltpu.VMEM((half, depth, lanes), BF16),
            pltpu.VMEM((half, depth, lanes), BF16),
            pltpu.VMEM((half, depth, lanes), BF16),
            pltpu.VMEM((half, depth, lanes), BF16),
            pltpu.VMEM((depth, lanes), BF16),
            pltpu.VMEM((depth, lanes), BF16),
            pltpu.VMEM((rows, width), F32),
            pltpu.VMEM((rows, width), F32),
            pltpu.VMEM((parts, n, slot_rows, width // parts // pieces), BF16),
            pltpu.VMEM((parts, n, slot_rows, width // parts // pieces), BF16),
            pltpu.SemaphoreType.DMA((5,)),
            sems,
            sems,
            half_sems,
            half_sems,
            half_sems,
            half_sems,
            pltpu.SemaphoreType.DMA((2,)),
            pltpu.SemaphoreType.DMA((parts, n)),
            pltpu.SemaphoreType.DMA((parts, n)),
        ],
        compiler_params=pltpu.CompilerParams(
            collective_id=0, has_side_effects=True, vmem_limit_bytes=VMEM_LIMIT
        ),
        cost_estimate=pl.CostEstimate(
            flops=flops, bytes_accessed=12 * 1024 * 1024, transcendentals=1024 * 1024
        ),
    )(
        features,
        state_write.T,
        state_read.T,
        log_decay.T,
        skip_gain[None, :],
        post_gain[None, :],
        start_index[None, :],
        value_weight.reshape(-1, 128),
        step_noise,
        act_weight,
        dyn_weight,
        act_in_weight,
        out_weight,
    )
    return pl.pallas_call(
        hand_over,
        out_shape=tuple(jax.ShapeDtypeStruct(r.shape, r.dtype) for r in results),
        in_specs=[vmem] * 3,
        out_specs=(hbm, hbm, hbm),
        scratch_shapes=[pltpu.SemaphoreType.DMA((3,))],
    )(*results)


def solution(mesh):
    split = P(("groups", "seq"), None)
    placed = (
        split,
        split,
        split,
        split,
        P(),
        P(),
        P(("groups", "seq")),
        P(None, ("groups", "seq"), None),
        P(),
        P(),
        P(),
        P(),
        P(),
    )
    return jax.shard_map(
        per_device,
        mesh=mesh,
        in_specs=placed,
        out_specs=(split, P(None, ("groups", "seq")), split),
        check_vma=False,
    )
```

```python
import functools
import jax
import jax.numpy as jnp
from jax import lax
from jax.experimental import pallas as pl
from jax.experimental.pallas import tpu as pltpu
from jax.sharding import PartitionSpec as P

F32 = jnp.float32
BF16 = jnp.bfloat16
VMEM_LIMIT = 56 * 1024 * 1024


def dot(a, b):
    return jnp.dot(a, b, preferred_element_type=F32)


def dot_nt(a, b):
    return lax.dot_general(a, b, (((1,), (1,)), ((), ())), preferred_element_type=F32)


def iota(shape, dim):
    return lax.broadcasted_iota(jnp.int32, shape, dim)


def plan(n, rows, width, state, starts):
    half = n // 2
    lanes = max(128, width // half)
    lane_blocks = width // lanes
    cuts = min(state // 16, half // lane_blocks)
    assert lane_blocks * cuts == half
    cap = starts // n
    pieces = max(1, 16 // cap)
    parts = 2 if width // 2 // pieces >= 128 and lane_blocks % 2 == 0 else 1
    return lanes, lane_blocks, cuts, cap, pieces, parts


def kernel(
    n,
    x_ref,
    write_ref,
    read_ref,
    decay_ref,
    skip_ref,
    gain_ref,
    start_ref,
    value_w_ref,
    noise_hbm,
    act_hbm,
    dyn_hbm,
    act_in_hbm,
    out_hbm,
    post,
    values_ref,
    latent,
    noise,
    act_w,
    dyn_w,
    act_in_w,
    out_w,
    meta_out,
    meta_in,
    end_out,
    end_in,
    carry_out,
    carry_in,
    cross_out,
    cross_in,
    local,
    entered,
    pick_out,
    pick_in,
    load_sem,
    meta_s,
    meta_r,
    end_s,
    end_r,
    carry_s,
    carry_r,
    cross_sem,
    pick_s,
    pick_r,
):
    rows, width = x_ref.shape
    heads = decay_ref.shape[0]
    state = write_ref.shape[0]
    starts = start_ref.shape[1]
    lanes, lane_blocks, cuts, cap, pieces, parts = plan(n, rows, width, state, starts)
    head_width = width // heads
    half = n // 2
    depth = state // cuts
    slot_rows = pieces * cap
    part_width = width // parts
    piece_width = part_width // pieces
    me = lax.axis_index("seq")
    upper = me // half
    mine = lax.rem(me, half)
    base_of_half = upper * half

    def far_first(i):
        step = n // 2 + (i + 1) // 2 * (2 * lax.rem(i, 2) - 1)
        return lax.rem(me + step, n)

    loads = [
        pltpu.make_async_copy(src, dst, load_sem.at[i])
        for i, (src, dst) in enumerate(
            (
                (act_hbm, act_w),
                (dyn_hbm, dyn_w),
                (act_in_hbm, act_in_w),
                (out_hbm, out_w),
                (noise_hbm, noise),
            )
        )
    ]
    for load in loads:
        load.start()

    barrier = pltpu.get_barrier_semaphore()

    def greet(j, _):
        pl.semaphore_signal(
            barrier,
            inc=1,
            device_id={"seq": lax.rem(me + j, n)},
            device_id_type=pl.DeviceIdType.MESH,
        )
        return 0

    lax.fori_loop(1, n, greet, 0)

    def remote(src, dst, send, recv, peer, slot):
        return pltpu.make_async_remote_copy(
            src_ref=src,
            dst_ref=dst,
            send_sem=send.at[peer],
            recv_sem=recv.at[slot],
            device_id={"seq": peer},
            device_id_type=pl.DeviceIdType.MESH,
        )

    lower = iota((rows, rows), 0) >= iota((rows, rows), 1)
    running_t = jnp.dot(
        decay_ref[...],
        (iota((rows, rows), 0) <= iota((rows, rows), 1)).astype(F32),
        precision=lax.Precision.HIGHEST,
        preferred_element_type=F32,
    )
    running = running_t.T
    spread = (
        iota((2 * heads, width), 1) // head_width == lax.rem(iota((2 * heads, width), 0), heads)
    ).astype(BF16)

    def widen(v):
        high = v.astype(BF16).astype(F32)
        return dot(jnp.concatenate([high, v - high], axis=1).astype(BF16), spread)

    x_all = x_ref[...].astype(F32)
    tail = widen(jnp.exp(running[rows - 1 : rows] - running))
    end_state = dot(write_ref[...], (x_all * tail).astype(BF16))
    whole_decay = widen(jnp.exp(running[rows - 8 : rows]))[7:8]
    start_row = start_ref[...].astype(F32)
    for k in range(half):
        at = slice((k // cuts) * lanes, (k // cuts + 1) * lanes)
        end_out[k] = end_state[(k % cuts) * depth : (k % cuts + 1) * depth, at].astype(BF16)
    decay_rows = lanes // 128
    for k in range(n):
        first_lane = (k % half) // cuts * lanes
        meta_out[k, 0:1, :] = start_row
        for i in range(decay_rows):
            lane = first_lane + i * 128
            meta_out[k, 1 + i : 2 + i, :] = whole_decay[:, lane : lane + 128]

    pl.semaphore_wait(barrier, n - 1)

    def send_end(j, _):
        k = lax.rem(mine + j, half)
        pltpu.make_async_remote_copy(
            src_ref=end_out.at[k],
            dst_ref=end_in.at[mine],
            send_sem=end_s.at[k],
            recv_sem=end_r.at[mine],
            device_id={"seq": base_of_half + k},
            device_id_type=pl.DeviceIdType.MESH,
        ).start()
        return 0

    lax.fori_loop(1, half, send_end, 0)

    def send_meta(i, _):
        peer = far_first(i)
        remote(meta_out.at[peer], meta_in.at[me], meta_s, meta_r, peer, me).start()
        return 0

    lax.fori_loop(0, n - 1, send_meta, 0)
    meta_in[pl.ds(me, 1)] = meta_out[pl.ds(me, 1)]
    end_in[pl.ds(mine, 1)] = end_out[pl.ds(mine, 1)]

    eye_rows = (iota((rows, rows), 0) == iota((rows, rows), 1)).astype(BF16)
    read = dot_nt(eye_rows, read_ref[...]).astype(BF16)
    gram = dot(read, write_ref[...])
    skip = widen(jnp.broadcast_to(skip_ref[...], (8, heads)))[0:1]
    per_tile = 128 // head_width
    head_of = iota((rows, 128), 1) // head_width

    def local_tiles(tiles):
        for tile in tiles:
            at = slice(tile * 128, (tile + 1) * 128)
            x_tile = x_ref[:, at].astype(F32)
            total = x_tile * skip[:, at]
            for inner in range(per_tile):
                h = tile * per_tile + inner
                gap = running[:, h : h + 1] - running_t[h : h + 1, :]
                weight = (jnp.exp(jnp.where(lower, gap, -jnp.inf)) * gram).astype(BF16)
                one_head = jnp.where(head_of == inner, x_tile, 0.0).astype(BF16)
                total = total + dot(weight, one_head)
            local[:, at] = total

    tiles = width // 128
    local_tiles(range(tiles // 2))

    def wait_meta(d):
        remote(meta_out.at[0], meta_in.at[d], meta_s, meta_r, d, d).wait_recv()

    def ends_lap(j, _):
        k = lax.rem(mine + j, half)
        pltpu.make_async_remote_copy(
            src_ref=end_out.at[0],
            dst_ref=end_in.at[k],
            send_sem=end_s.at[k],
            recv_sem=end_r.at[k],
            device_id={"seq": base_of_half + k},
            device_id_type=pl.DeviceIdType.MESH,
        ).wait_recv()
        wait_meta(base_of_half + k)
        return 0

    lax.fori_loop(1, half, ends_lap, 0)

    across = pltpu.make_async_remote_copy(
        src_ref=cross_out,
        dst_ref=cross_in,
        send_sem=cross_sem.at[0],
        recv_sem=cross_sem.at[1],
        device_id={"seq": lax.rem(me + half, n)},
        device_id_type=pl.DeviceIdType.MESH,
    )

    @pl.when(upper == 0)
    def _():
        cross_in[...] = jnp.zeros_like(cross_in)

    @pl.when(upper == 1)
    def _():
        across.wait_recv()

    def fold(d, carry):
        carry_out[d] = carry.astype(BF16)
        decay = jnp.concatenate(
            [meta_in[base_of_half + d, 1 + i : 2 + i, :] for i in range(decay_rows)], axis=1
        )
        return carry * decay + end_in[d].astype(F32)

    cross_out[...] = lax.fori_loop(0, half, fold, cross_in[...].astype(F32)).astype(BF16)

    @pl.when(upper == 0)
    def _():
        across.start()

    def send_carry(j, _):
        k = lax.rem(mine + j, half)
        pltpu.make_async_remote_copy(
            src_ref=carry_out.at[k],
            dst_ref=carry_in.at[mine],
            send_sem=carry_s.at[k],
            recv_sem=carry_r.at[mine],
            device_id={"seq": base_of_half + k},
            device_id_type=pl.DeviceIdType.MESH,
        ).start()
        return 0

    lax.fori_loop(1, half, send_carry, 0)
    carry_in[pl.ds(mine, 1)] = carry_out[pl.ds(mine, 1)]

    local_tiles(range(tiles // 2, tiles))
    entered[...] = widen(jnp.exp(running))

    def metas_lap(j, _):
        wait_meta(lax.rem(base_of_half + half + j, n))
        return 0

    lax.fori_loop(0, half, metas_lap, 0)

    asked = meta_in[:, 0, :starts]
    base = (me * rows).astype(F32)
    hit = jnp.logical_and(asked >= base, asked < base + rows)
    up_to = (iota((starts, starts), 0) <= iota((starts, starts), 1)).astype(BF16)
    rank = dot(hit.astype(F32).astype(BF16), up_to)
    rank = jnp.where(hit, rank, 0.0).astype(BF16)
    offset = jnp.where(hit, asked - base, 0.0).astype(BF16)
    slots = n * slot_rows
    repeat = (iota((slots, n), 0) // slot_rows == iota((slots, n), 1)).astype(BF16)
    slot_at = iota((slots, starts), 0)
    chosen = dot(repeat, rank) == (slot_at % cap + 1).astype(F32)
    wanted = jnp.sum(jnp.where(chosen, dot(repeat, offset), 0.0), axis=1, keepdims=True)
    row_at = iota((slots, rows), 0)
    picks_row = wanted == iota((slots, rows), 1).astype(F32)
    picks = [
        jnp.where(jnp.logical_and(picks_row, (row_at // cap) % pieces == p), 1.0, 0.0).astype(BF16)
        for p in range(pieces)
    ]

    start_col = jnp.sum(
        jnp.where(iota((starts, starts), 0) == iota((starts, starts), 1), start_row, 0.0),
        axis=1,
        keepdims=True,
    )
    first = (iota((starts, n), 1) * rows).astype(F32)
    from_owner = jnp.logical_and(start_col >= first, start_col < first + rows)
    before = (iota((starts, starts), 0) >= iota((starts, starts), 1)).astype(BF16)
    count = dot(before, from_owner.astype(F32).astype(BF16))
    lands = jnp.sum(
        jnp.where(from_owner, count - 1.0 + (iota((starts, n), 1) * slot_rows).astype(F32), 0.0),
        axis=1,
        keepdims=True,
    )

    def carry_lap(k, _):
        @pl.when(k != mine)
        def _():
            pltpu.make_async_remote_copy(
                src_ref=carry_out.at[0],
                dst_ref=carry_in.at[k],
                send_sem=carry_s.at[k],
                recv_sem=carry_r.at[k],
                device_id={"seq": base_of_half + k},
                device_id_type=pl.DeviceIdType.MESH,
            ).wait_recv()

        return 0

    same_head = jnp.where(
        iota((lanes, lanes), 0) // head_width == iota((lanes, lanes), 1) // head_width,
        1.0 / head_width,
        0.0,
    ).astype(BF16)
    for part in range(parts):
        lax.fori_loop(part * half // parts, (part + 1) * half // parts, carry_lap, 0)
        for block in range(part * lane_blocks // parts, (part + 1) * lane_blocks // parts):
            at = slice(block * lanes, (block + 1) * lanes)
            carry = carry_in[block * cuts : (block + 1) * cuts].reshape(state, lanes)
            mixed = local[:, at] + dot(read, carry) * entered[:, at]
            square_mean = dot((mixed * mixed).astype(BF16), same_head)
            post[:, at] = (mixed * lax.rsqrt(square_mean + 1e-05) * gain_ref[:, at]).astype(BF16)
        picked = 0.0
        for p in range(pieces):
            lane = part * part_width + p * piece_width
            picked = picked + dot(picks[p], post[:, lane : lane + piece_width])
        pick_out[part] = picked.astype(BF16).reshape(n, slot_rows, piece_width)

        def send_rows(i, _):
            peer = far_first(i)
            remote(
                pick_out.at[part, peer],
                pick_in.at[part, me],
                pick_s.at[part],
                pick_r.at[part],
                peer,
                me,
            ).start()
            return 0

        lax.fori_loop(0, n - 1, send_rows, 0)
        pick_in[part, pl.ds(me, 1)] = pick_out[part, pl.ds(me, 1)]
    for load in loads:
        load.wait()

    slot_of = iota((starts, slots), 1).astype(F32)
    act_sum, dyn_sum = 0.0, 0.0
    for part in range(parts):

        def row_lap(j, _):
            peer = lax.rem(me + j, n)
            remote(
                pick_out.at[part, 0],
                pick_in.at[part, peer],
                pick_s.at[part],
                pick_r.at[part],
                peer,
                peer,
            ).wait_recv()
            return 0

        lax.fori_loop(1, n, row_lap, 0)
        landed = pick_in[part].reshape(slots, piece_width)
        for p in range(pieces):
            place = jnp.where(slot_of == lands + float(p * cap), 1.0, 0.0).astype(BF16)
            lane = part * part_width + p * piece_width
            latent[:, lane : lane + piece_width] = dot(place, landed).astype(BF16)
        at = slice(part * part_width, (part + 1) * part_width)
        act_sum = act_sum + dot(latent[:, at], act_w[at, :])
        dyn_sum = dyn_sum + dot(latent[:, at], dyn_w[at, :])

    diagonal = iota((starts, starts), 0) == iota((starts, starts), 1)
    value_rows = value_w_ref[...].astype(F32)
    value_w = jnp.concatenate(
        [value_rows[i : i + 1] for i in range(value_rows.shape[0])], axis=1
    )
    for step in range(noise.shape[0]):
        wide = latent[...].astype(F32)
        scale = lax.rsqrt(jnp.mean(wide * wide, axis=-1, keepdims=True) + 1e-06)
        if step > 0:
            act_sum = dot(latent[...], act_w[...])
            dyn_sum = dot(latent[...], dyn_w[...])
        action = jnp.tanh(act_sum * scale).astype(BF16)
        inner = dyn_sum * scale + dot(action, act_in_w[...])
        hidden = (inner / (1.0 + jnp.exp(-inner)) + noise[step].astype(F32)).astype(BF16)
        value = jnp.sum(hidden.astype(F32) * value_w, axis=1, keepdims=True)
        values_ref[step : step + 1, :] = jnp.sum(
            jnp.where(diagonal, value, 0.0), axis=0, keepdims=True
        )
        latent[...] = (wide + dot(hidden, out_w[...])).astype(BF16)

    def sent(j, _):
        peer = lax.rem(me + j, n)
        remote(meta_out.at[0], meta_in.at[me], meta_s, meta_r, peer, me).wait_send()
        for part in range(parts):
            remote(
                pick_out.at[part, 0],
                pick_in.at[part, me],
                pick_s.at[part],
                pick_r.at[part],
                peer,
                me,
            ).wait_send()

        return 0

    lax.fori_loop(1, n, sent, 0)

    def sent_in_half(j, _):
        k = lax.rem(mine + j, half)
        for src, dst, send, recv in (
            (end_out, end_in, end_s, end_r),
            (carry_out, carry_in, carry_s, carry_r),
        ):
            pltpu.make_async_remote_copy(
                src_ref=src.at[0],
                dst_ref=dst.at[mine],
                send_sem=send.at[k],
                recv_sem=recv.at[mine],
                device_id={"seq": base_of_half + k},
                device_id_type=pl.DeviceIdType.MESH,
            ).wait_send()
        return 0

    lax.fori_loop(1, half, sent_in_half, 0)

    @pl.when(upper == 0)
    def _():
        across.wait_send()


def hand_over(*refs):
    sem = refs[6]
    copies = [pltpu.make_async_copy(refs[i], refs[3 + i], sem.at[i]) for i in range(3)]
    for copy in copies:
        copy.start()
    for copy in copies:
        copy.wait()


def per_device(
    features,
    state_write,
    state_read,
    log_decay,
    skip_gain,
    post_gain,
    start_index,
    step_noise,
    act_weight,
    dyn_weight,
    act_in_weight,
    out_weight,
    value_weight,
):
    n = lax.axis_size("seq")
    rows, width = features.shape
    state = state_write.shape[1]
    starts = start_index.shape[0]
    lanes, lane_blocks, cuts, cap, pieces, parts = plan(n, rows, width, state, starts)
    half, depth, slot_rows = n // 2, state // cuts, pieces * cap
    vmem = pl.BlockSpec(memory_space=pltpu.VMEM)
    hbm = pl.BlockSpec(memory_space=pl.ANY)
    sems = pltpu.SemaphoreType.DMA((n,))
    half_sems = pltpu.SemaphoreType.DMA((half,))
    flops = 2 * step_noise.shape[0] * starts * (dyn_weight.size + out_weight.size)
    results = pl.pallas_call(
        functools.partial(kernel, n),
        out_shape=(
            pltpu.VMEM((rows, width), BF16),
            pltpu.VMEM((step_noise.shape[0], starts), F32),
            pltpu.VMEM((starts, width), BF16),
        ),
        in_specs=[vmem] * 8 + [hbm] * 5,
        out_specs=(vmem, vmem, vmem),
        scratch_shapes=[
            pltpu.VMEM(step_noise.shape, BF16),
            pltpu.VMEM(act_weight.shape, BF16),
            pltpu.VMEM(dyn_weight.shape, BF16),
            pltpu.VMEM(act_in_weight.shape, BF16),
            pltpu.VMEM(out_weight.shape, BF16),
            pltpu.VMEM((n, 8, 128), F32),
            pltpu.VMEM((n, 8, 128), F32),
            pltpu.VMEM((half, depth, lanes), BF16),
            pltpu.VMEM((half, depth, lanes), BF16),
            pltpu.VMEM((half, depth, lanes), BF16),
            pltpu.VMEM((half, depth, lanes), BF16),
            pltpu.VMEM((depth, lanes), BF16),
            pltpu.VMEM((depth, lanes), BF16),
            pltpu.VMEM((rows, width), F32),
            pltpu.VMEM((rows, width), F32),
            pltpu.VMEM((parts, n, slot_rows, width // parts // pieces), BF16),
            pltpu.VMEM((parts, n, slot_rows, width // parts // pieces), BF16),
            pltpu.SemaphoreType.DMA((5,)),
            sems,
            sems,
            half_sems,
            half_sems,
            half_sems,
            half_sems,
            pltpu.SemaphoreType.DMA((2,)),
            pltpu.SemaphoreType.DMA((parts, n)),
            pltpu.SemaphoreType.DMA((parts, n)),
        ],
        compiler_params=pltpu.CompilerParams(
            collective_id=0, has_side_effects=True, vmem_limit_bytes=VMEM_LIMIT
        ),
        cost_estimate=pl.CostEstimate(
            flops=flops, bytes_accessed=12 * 1024 * 1024, transcendentals=1024 * 1024
        ),
    )(
        features,
        state_write.T,
        state_read.T,
        log_decay.T,
        skip_gain[None, :],
        post_gain[None, :],
        start_index[None, :],
        value_weight.reshape(-1, 128),
        step_noise,
        act_weight,
        dyn_weight,
        act_in_weight,
        out_weight,
    )
    return pl.pallas_call(
        hand_over,
        out_shape=tuple(jax.ShapeDtypeStruct(r.shape, r.dtype) for r in results),
        in_specs=[vmem] * 3,
        out_specs=(hbm, hbm, hbm),
        scratch_shapes=[pltpu.SemaphoreType.DMA((3,))],
        compiler_params=pltpu.CompilerParams(vmem_limit_bytes=VMEM_LIMIT // 7),
    )(*results)


def solution(mesh):
    split = P(("groups", "seq"), None)
    placed = (
        split,
        split,
        split,
        split,
        P(),
        P(),
        P(("groups", "seq")),
        P(None, ("groups", "seq"), None),
        P(),
        P(),
        P(),
        P(),
        P(),
    )
    return jax.shard_map(
        per_device,
        mesh=mesh,
        in_specs=placed,
        out_specs=(split, P(None, ("groups", "seq")), split),
        check_vma=False,
    )
```
